256 devices in a mesh: loop: 16 (over x_hi, y, core), inner: 16 (over z, x_lo).
Axes of the slice: x: 4 (x_hi: 2, x_lo: 2; x = x_hi * 2 + x_lo), y: 4, z: 8, core: 2. Of those that a mesh axis runs over, the one named last changes fastest.
Arguments:
- images: bfloat16 [32768, 1536], P(('loop', 'inner')), may hold values from -0.75 to 0.75
- texts: bfloat16 [32768, 1536], P(('loop', 'inner')), may hold values from -0.75 to 0.75
- labels: int32 [32768], P(('loop', 'inner')), may hold values from 0 to 127
- scale: float32 [1], replicated, may hold values from 1 to 4
- bias: float32 [1], replicated, may hold values from -4 to -1
Outputs:
- loss: float32 [1], replicated
- grad_images: float32 [32768, 1536], P(('loop', 'inner'))
- grad_texts: float32 [32768, 1536], P(('loop', 'inner'))
The draws below stay inside these ranges and needn't reach their ends.
All inputs are finite; a program needn't handle non-finite values.
Results may differ from the reference program's by a relative error of at most 0.0015.
The reference program's roundings to bfloat16 on the way count: a program that leaves them out, or rounds other values in their place, can miss the bound.
Values may be sent and summed in bfloat16 or wider, within the bound.
No kernel may reach another device: no remote copies, remote signals or barrier semaphores. Data moves between devices by JAX's collectives and lax.ppermute only.
A program may use at most 128 MiB of HBM per device.

```python
import math
import jax
import jax.numpy as jnp
from jax import lax

D = 1536
ROWS_DEV = 128
REACH = 2
B = 32768
COLS = 10240
N_LOOP = 16
N_INNER = 16


def touch_ends(drawn, stream_key, low, high):
    index_at = [jax.random.randint(jax.random.fold_in(stream_key, axis), (), 0, length) for axis, length in enumerate(drawn.shape)]
    widest = drawn.shape.index(max(drawn.shape))
    next_to = index_at[:widest] + [(index_at[widest] + 1) % drawn.shape[widest]] + index_at[widest + 1:]
    return drawn.at[tuple(index_at)].set(low).at[tuple(next_to)].set(high)


def block_levels(own_key, extent, split, least, top_value):
    gain = 1.0
    for dim, blocks in split:
        heights = jax.random.uniform(jax.random.fold_in(jax.random.fold_in(own_key, 6), dim), (blocks,), jnp.float32, least / len(split), top_value / len(split))
        gain = gain * jnp.repeat(jnp.exp(heights), extent[dim] // blocks).reshape((-1,) + (1,) * (len(extent) - 1 - dim))
    return gain


def bell_draw(own_key, extent, deviation, limit, pieces=(), kind=jnp.bfloat16):
    result = jax.random.normal(own_key, extent, jnp.float32) * deviation
    if len(pieces) > 0:
        result = block_levels(own_key, extent, pieces, -0.22, 0.18) * result
    return jnp.clip(result, min=-limit, max=limit).astype(kind)


def setup_inputs(seed: int = 0) -> dict:
    splits = jax.random.split(jax.random.key(seed), 6)
    images = bell_draw(splits[0], (B, D), 0.125, 0.75, ((0, 256),))
    texts = bell_draw(splits[1], (B, D), 0.125, 0.75, ((0, 256),))
    labels = touch_ends(jax.random.randint(splits[2], (B,), 0, ROWS_DEV), jax.random.fold_in(splits[2], 1), 0, ROWS_DEV - 1).astype(jnp.int32)
    scale = jnp.clip(jnp.exp(jax.random.uniform(splits[3], (1,), jnp.float32, math.log(1.0), math.log(4.0))), 1.0, 4.0)
    bias = jnp.clip(jax.random.uniform(splits[4], (1,), jnp.float32, -4.0, -1.0), -4.0, -1.0)
    return {"images": images, "texts": texts, "labels": labels, "scale": scale, "bias": bias}


def pairwise_terms(picture_block_local, label_signs, caption_rows, logit_scale_factor, logit_offset_term):
    score_matrix = logit_scale_factor * lax.dot_general(picture_block_local, caption_rows, (((1,), (1,)), ((), ())), preferred_element_type=jnp.float32) + logit_offset_term
    loss_piece = jnp.sum(jax.nn.softplus(-label_signs * score_matrix))
    sigmoid_weights = (-label_signs * jax.nn.sigmoid(-label_signs * score_matrix)).astype(jnp.bfloat16)
    picture_gradient = logit_scale_factor * jnp.dot(sigmoid_weights, caption_rows, preferred_element_type=jnp.float32)
    caption_gradient = logit_scale_factor * lax.dot_general(sigmoid_weights, picture_block_local, (((0,), (0,)), ((), ())), preferred_element_type=jnp.float32)
    return loss_piece, picture_gradient, caption_gradient


def reference(images, texts, labels, scale, bias):
    logit_scale_factor = scale[0]
    logit_offset_term = bias[0]
    group_size = ROWS_DEV * N_INNER
    columns = jnp.arange(group_size, dtype=jnp.int32)
    negative_pairs = jnp.full((group_size, group_size), -1.0, jnp.float32)

    def visit(carry, block_index):
        text_total, loss_total = carry
        start = (block_index * group_size).astype(jnp.int32)
        picture_block_local = lax.dynamic_slice_in_dim(images, start, group_size, 0)
        label_block = lax.dynamic_slice_in_dim(labels, start, group_size, 0)
        target = (columns // ROWS_DEV) * ROWS_DEV + label_block
        positive_pairs = jnp.where(columns[None, :] == target[:, None], jnp.float32(1.0), jnp.float32(-1.0))
        picture_gradient = jnp.zeros((group_size, D), jnp.float32)
        for offset in range(-REACH, REACH + 1):
            text_start = (((block_index + offset) % N_LOOP) * group_size).astype(jnp.int32)
            caption_rows = lax.dynamic_slice_in_dim(texts, text_start, group_size, 0)
            label_signs = positive_pairs if offset == 0 else negative_pairs
            loss_piece, gradient_piece, caption_gradient = pairwise_terms(picture_block_local, label_signs, caption_rows, logit_scale_factor, logit_offset_term)
            picture_gradient = picture_gradient + gradient_piece
            loss_total = loss_total + loss_piece
            current = lax.dynamic_slice_in_dim(text_total, text_start, group_size, 0)
            text_total = lax.dynamic_update_slice_in_dim(text_total, current + caption_gradient, text_start, 0)
        return (text_total, loss_total), picture_gradient

    start_carry = (jnp.zeros((B, D), jnp.float32), jnp.zeros((), jnp.float32))
    (grad_texts, loss_sum), image_blocks = lax.scan(visit, start_carry, jnp.arange(N_LOOP, dtype=jnp.int32))
    grad_images = image_blocks.reshape(B, D)
    loss = (loss_sum / (jnp.float32(B) * jnp.float32(COLS))).reshape(1)
    return loss, grad_images, grad_texts
```

```python
import functools
import jax
import jax.numpy as jnp
from jax import lax
from jax.experimental import pallas as pl
from jax.experimental.pallas import tpu as pltpu
from jax.sharding import PartitionSpec as P

AXES = ("loop", "inner")
N_LOOP, N_INNER = 16, 16
N_Z = 8
ROWS = 128
HALF = 64
WIDTH = 1536
CODE_WIDTH = WIDTH + 128
GROUPS = 5
IMAGES = GROUPS * 2 * ROWS
TEXTS = N_Z * ROWS
EARLY = TEXTS - ROWS
MIB = 1024 * 1024


def pairs(move):
    out = []
    for loop in range(N_LOOP):
        for inner in range(N_INNER):
            chip, core, z, side = loop // 2, loop % 2, inner // 2, inner % 2
            to_chip, to_core, to_z, to_side = move(chip, core, z, side)
            out.append(
                (
                    loop * N_INNER + inner,
                    ((to_chip % 8) * 2 + to_core) * N_INNER + (to_z % N_Z) * 2 + to_side,
                )
            )
    return out


Z_UP = pairs(lambda c, k, z, s: (c, k, z + 1, s))
Z_DOWN = pairs(lambda c, k, z, s: (c, k, z - 1, s))
CHIP_UP = pairs(lambda c, k, z, s: (c + 1, k, z, s))
CHIP_DOWN = pairs(lambda c, k, z, s: (c - 1, k, z, s))
SIDE = pairs(lambda c, k, z, s: (c, k, z, 1 - s))
CORE = pairs(lambda c, k, z, s: (c, 1 - k, z, s))
FLIPS = (
    CORE,
    SIDE,
    pairs(lambda c, k, z, s: (c ^ 1, k, z, s)),
    pairs(lambda c, k, z, s: (c ^ 2, k, z, s)),
    pairs(lambda c, k, z, s: (c ^ 4, k, z, s)),
    pairs(lambda c, k, z, s: (c, k, z ^ 1, s)),
    pairs(lambda c, k, z, s: (c, k, z ^ 2, s)),
    pairs(lambda c, k, z, s: (c, k, z ^ 4, s)),
)


def send(array, route):
    return lax.ppermute(array, AXES, route)


def vmem(array):
    return pltpu.with_memory_space_constraint(array, pltpu.VMEM)


VM = pl.BlockSpec(memory_space=pltpu.VMEM)
SM = pl.BlockSpec(memory_space=pltpu.SMEM)


def kernel_call(body, outs, args, scratch=(), aliases=None, flops=0, limit=16):
    specs = [SM if a.ndim == 1 else VM for a in args]
    args = [a if a.ndim == 1 else vmem(a) for a in args]
    return pl.pallas_call(
        body,
        out_shape=tuple(pltpu.VMEM(s, d) for s, d in outs),
        in_specs=specs,
        out_specs=tuple(VM for _ in outs),
        scratch_shapes=list(scratch),
        input_output_aliases=aliases or {},
        compiler_params=pltpu.CompilerParams(vmem_limit_bytes=limit * MIB),
        cost_estimate=pl.CostEstimate(flops=flops, bytes_accessed=0, transcendentals=0),
    )(*args)


def encode(value, code_ref, rows):
    top = jnp.max(jnp.abs(value), axis=1, keepdims=True)
    power = jnp.floor(jnp.log2(jnp.maximum(top, 1e-30))) - 13.0
    code = jnp.round(value * jnp.exp2(-power)).astype(jnp.int32)
    code_ref[rows, :WIDTH] = code.astype(jnp.int16)
    code_ref[rows, WIDTH:] = jnp.broadcast_to(
        power.astype(jnp.int32), (value.shape[0], 128)
    ).astype(jnp.int16)


def decode(code_ref, rows):
    power = code_ref[rows, WIDTH:].astype(jnp.int32).astype(jnp.float32)[:, :1]
    return code_ref[rows, :WIDTH].astype(jnp.int32).astype(jnp.float32) * jnp.exp2(power)


def pair_terms(logits, positive):
    signed = logits if positive is None else jnp.where(positive, -logits, logits)
    small = jnp.exp(-jnp.abs(signed))
    whole = 1.0 + small
    weight = jnp.where(signed >= 0, 1.0, small) / whole
    series = small * (1.0 - small * (0.5 - small * (1.0 / 3.0)))
    loss = jnp.maximum(signed, 0.0) + jnp.where(small < 0.01, series, jnp.log(whole))
    if positive is not None:
        weight = jnp.where(positive, -weight, weight)
    return loss, weight.astype(jnp.bfloat16)


def weigh(text, image_ref, out_ref, base, scale, bias, labels, scores):
    rows = text.shape[0]
    total = jnp.zeros((8, 256), jnp.float32)
    for group in range(GROUPS):
        columns = slice(group * 256, group * 256 + 256)
        scores[:rows] = lax.dot_general(
            text, image_ref[columns, :], (((1,), (1,)), ((), ())), preferred_element_type=jnp.float32
        )
        for start in range(0, rows, 64):
            logits = scale * scores[start : start + 64] + bias
            positive = None
            if labels is not None and group == 0 and start < ROWS:
                row = start + lax.broadcasted_iota(jnp.int32, (64, 256), 0)
                positive = row == labels
            loss, weight = pair_terms(logits, positive)
            out_ref[base + start : base + start + 64, columns] = weight
            total = total + jnp.sum(loss.reshape(8, 8, 256), axis=0)
    return total[:, :128] + total[:, 128:]


def early_body(scale, bias, labels, *refs):
    images, texts = refs[:10], refs[10:23]
    weights, image_all, text_all, loss, scores = refs[23:]
    for i, ref in enumerate(images):
        image_all[i * ROWS : i * ROWS + ROWS, :] = ref[...]
    at = 0
    for ref in texts:
        text_all[at : at + ref.shape[0], :] = ref[...]
        at += ref.shape[0]
    loss[...] = weigh(
        text_all[:EARLY, :], image_all, weights, 0, scale[0], bias[0], labels[...], scores
    )


def late_body(scale, bias, first, second, image_all, weights_in, text_in, weights, text_all, loss, code_a, code_b, scores):
    del weights_in, text_in
    text_all[EARLY : EARLY + HALF, :] = first[...]
    text_all[EARLY + HALF :, :] = second[...]
    loss[...] = weigh(
        text_all[EARLY:, :], image_all, weights, EARLY, scale[0], bias[0], None, scores
    )
    grad = jnp.dot(weights[EARLY:, :], image_all[...], preferred_element_type=jnp.float32)
    encode(grad[:HALF], code_a, slice(0, HALF))
    encode(grad[HALF:], code_b, slice(0, HALF))


def text_grad_body(start, rows, weights, image_all, out):
    out[...] = jnp.dot(
        weights[start : start + rows, :], image_all[...], preferred_element_type=jnp.float32
    )


def add_body(at, part, code, out):
    encode(part[at : at + HALF, :] + decode(code, slice(0, HALF)), out, slice(0, HALF))


def fresh_body(at, part, out):
    encode(part[at : at + HALF, :], out, slice(0, HALF))


def text_final_body(scale, part, a_up, b_up, a_down, b_down, out):
    for at, one, two in ((0, a_up, a_down), (HALF, b_up, b_down)):
        rows = slice(0, HALF)
        out[at : at + HALF, :] = scale[0] * (
            part[at : at + HALF, :] + decode(one, rows) + decode(two, rows)
        )


def image_grad(weights, text_all, group):
    return lax.dot_general(
        weights[:, group * 256 : group * 256 + 256],
        text_all[...],
        (((0,), (0,)), ((), ())),
        preferred_element_type=jnp.float32,
    )


def image_code_body(weights, text_all, *outs):
    for i, group in enumerate((1, 4)):
        grad = image_grad(weights, text_all, group)
        for slot in range(2):
            encode(grad[slot * ROWS : slot * ROWS + ROWS], outs[2 * i + slot], slice(0, ROWS))


def image_keep_body(weights, text_all, own, up, down):
    for group, ref in ((0, own), (2, up), (3, down)):
        ref[...] = image_grad(weights, text_all, group)


def chip_body(slot, core, up, down, code, up_out, down_out):
    rows = slice(slot * ROWS, slot * ROWS + ROWS)
    extra = decode(code, slice(0, ROWS))
    first = (core[0] == 0).astype(jnp.float32)
    encode(up[rows, :] + (1.0 - first) * extra, up_out, slice(0, ROWS))
    encode(down[rows, :] + first * extra, down_out, slice(0, ROWS))


def side_body(own, other, one, two, out):
    rows = slice(0, ROWS)
    encode(
        own[ROWS:, :] + decode(other, rows) + decode(one, rows) + decode(two, rows), out, rows
    )


def image_final_body(scale, own, other, one, two, side, out):
    rows = slice(0, ROWS)
    out[...] = scale[0] * (
        own[:ROWS, :]
        + decode(other, rows)
        + decode(one, rows)
        + decode(two, rows)
        + decode(side, rows)
    )


CODE = ((HALF, CODE_WIDTH), jnp.int16)
CODE2 = ((ROWS, CODE_WIDTH), jnp.int16)
BF, F32 = jnp.bfloat16, jnp.float32
UNIT_FLOPS = 2 * ROWS * ROWS * WIDTH


def on_device(images, texts, labels, scale, bias):
    core = lax.rem(lax.axis_index("loop"), 2).reshape(1)
    up = [texts[:HALF], texts[HALF:]]
    down = list(up)
    own = [images, send(images, SIDE)]
    ring = {}
    for step in range(1, 5):
        for i in range(2):
            if step < 4 or i == 0:
                up[i] = send(up[i], Z_UP)
                ring["u", step, i] = up[i]
            j = 1 - i
            if step < 4 or j == 1:
                down[j] = send(down[j], Z_DOWN)
                ring["d", step, j] = down[j]
    from_up = [send(a, CHIP_UP) for a in own]
    from_down = [send(a, CHIP_DOWN) for a in own]
    other = [send(a, CORE) for a in own]
    across = [
        send(jnp.where(core == 0, a, b), CORE) for a, b in zip(from_down, from_up)
    ]
    text_list = [texts]
    for step in (1, 2, 3):
        for way in "ud":
            text_list += [ring[way, step, 0], ring[way, step, 1]]
    label_row = jnp.concatenate([labels, jnp.full((ROWS,), -1, jnp.int32)]).reshape(1, 256)
    scores = pltpu.VMEM((EARLY, 256), F32)
    weights, image_all, text_all, loss_a = kernel_call(
        early_body,
        [((TEXTS, IMAGES), BF), ((IMAGES, WIDTH), BF), ((TEXTS, WIDTH), BF), ((8, 128), F32)],
        [scale, bias, label_row, *own, *other, *from_up, *from_down, *across, *text_list],
        scratch=[scores],
        flops=70 * UNIT_FLOPS,
        limit=32,
    )
    weights, text_all, loss_b, code_a, code_b = kernel_call(
        late_body,
        [((TEXTS, IMAGES), BF), ((TEXTS, WIDTH), BF), ((8, 128), F32), CODE, CODE],
        [scale, bias, ring["u", 4, 0], ring["d", 4, 1], image_all, weights, text_all],
        scratch=[pltpu.VMEM((ROWS, 256), F32)],
        aliases={5: 0, 6: 1},
        flops=20 * UNIT_FLOPS,
        limit=32,
    )
    back = {("u", 0): send(code_a, Z_DOWN), ("d", 1): send(code_b, Z_UP)}
    codes = kernel_call(
        image_code_body, [CODE2] * 4, [weights, text_all], flops=32 * UNIT_FLOPS, limit=32
    )
    crossed = [send(a, CORE) for a in codes]
    far = kernel_call(
        functools.partial(text_grad_body, 5 * ROWS, 2 * ROWS),
        [((2 * ROWS, WIDTH), F32)],
        [weights, image_all],
        flops=20 * UNIT_FLOPS,
        limit=32,
    )[0]
    rest = kernel_call(
        functools.partial(text_grad_body, 0, 5 * ROWS),
        [((5 * ROWS, WIDTH), F32)],
        [weights, image_all],
        flops=50 * UNIT_FLOPS,
        limit=32,
    )[0]
    keep = kernel_call(
        image_keep_body,
        [((256, WIDTH), F32)] * 3,
        [weights, text_all],
        flops=48 * UNIT_FLOPS,
        limit=32,
    )

    def part(way, step):
        return (far, 0 if way == "u" else ROWS) if step == 3 else (
            rest, (2 * step - 1) * ROWS if way == "u" else 2 * step * ROWS
        )

    route = {"u": Z_DOWN, "d": Z_UP}
    for way, half in (("u", 1), ("d", 0)):
        array, at = part(way, 3)
        code = kernel_call(
            functools.partial(fresh_body, at + half * HALF), [CODE], [array], limit=32
        )[0]
        back[way, half] = send(code, route[way])

    def hop(way, half, step):
        array, at = part(way, step)
        code = kernel_call(
            functools.partial(add_body, at + half * HALF), [CODE], [array, back[way, half]], limit=32
        )[0]
        back[way, half] = send(code, route[way])

    hop("u", 0, 3)
    hop("d", 1, 3)
    loss = loss_a + loss_b
    for flip in FLIPS:
        loss = loss + send(loss, flip)
    for step in (2, 1):
        hop("u", 1, step)
        hop("d", 0, step)
        hop("u", 0, step)
        hop("d", 1, step)
    returned = {}
    for slot in (1, 0):
        to_up, to_down = kernel_call(
            functools.partial(chip_body, slot),
            [CODE2] * 2,
            [core, keep[1], keep[2], crossed[2 + slot]],
            limit=32,
        )
        returned[slot] = (send(to_up, CHIP_DOWN), send(to_down, CHIP_UP))
    to_side = kernel_call(
        side_body, [CODE2], [keep[0], crossed[1], *returned[1]], limit=32
    )[0]
    from_side = send(to_side, SIDE)
    grad_images = kernel_call(
        image_final_body,
        [((ROWS, WIDTH), F32)],
        [scale, keep[0], crossed[0], *returned[0], from_side],
        limit=32,
    )[0]
    grad_texts = kernel_call(
        text_final_body,
        [((ROWS, WIDTH), F32)],
        [scale, rest, back["u", 0], back["u", 1], back["d", 0], back["d", 1]],
        limit=32,
    )[0]
    count = float(N_LOOP * N_INNER * ROWS) * float(GROUPS * N_INNER * ROWS)
    return (jnp.sum(loss) / count).reshape(1), grad_images, grad_texts


def solution(mesh):
    rows = P(AXES, None)
    return jax.shard_map(
        on_device,
        mesh=mesh,
        in_specs=(rows, rows, P(AXES), P(), P()),
        out_specs=(P(), rows, rows),
        check_vma=False,
    )
```

```python
import functools
import jax
import jax.numpy as jnp
from jax import lax
from jax.experimental import pallas as pl
from jax.experimental.pallas import tpu as pltpu
from jax.sharding import PartitionSpec as P

AXES = ("loop", "inner")
N_LOOP, N_INNER = 16, 16
N_Z = 8
ROWS = 128
HALF = 64
WIDTH = 1536
CODE_WIDTH = WIDTH + 128
GROUPS = 5
IMAGES = GROUPS * 2 * ROWS
TEXTS = N_Z * ROWS
EARLY = 5 * ROWS
LATE = 7 * ROWS
TOP = slice(0, HALF)
BOTTOM = slice(HALF, ROWS)
MIB = 1024 * 1024


def pairs(move):
    out = []
    for loop in range(N_LOOP):
        for inner in range(N_INNER):
            chip, core, z, side = loop // 2, loop % 2, inner // 2, inner % 2
            to_chip, to_core, to_z, to_side = move(chip, core, z, side)
            out.append(
                (
                    loop * N_INNER + inner,
                    ((to_chip % 8) * 2 + to_core) * N_INNER + (to_z % N_Z) * 2 + to_side,
                )
            )
    return out


def across_edge(index, first):
    return index + 1 if index % 2 == first else index - 1


Z_EVEN = pairs(lambda c, k, z, s: (c, k, across_edge(z, 0), s))
Z_ODD = pairs(lambda c, k, z, s: (c, k, across_edge(z, 1), s))
CHIP_EVEN = pairs(lambda c, k, z, s: (across_edge(c, 0), k, z, s))
CHIP_ODD = pairs(lambda c, k, z, s: (across_edge(c, 1), k, z, 1 - s if c % 4 in (0, 3) else s))
SIDE = pairs(lambda c, k, z, s: (c, k, z, 1 - s))
CORE = pairs(lambda c, k, z, s: (c, 1 - k, z, s))
ROW_FLIP = pairs(lambda c, k, z, s: (c ^ 2, k, z, s))
FAR_FLIP = pairs(lambda c, k, z, s: (c ^ 4, k, z, s))
Z_FLIP_2 = pairs(lambda c, k, z, s: (c, k, z ^ 2, s))
Z_FLIP_4 = pairs(lambda c, k, z, s: (c, k, z ^ 4, s))


def send(array, route):
    return lax.ppermute(array, AXES, route)


def vmem(array):
    return pltpu.with_memory_space_constraint(array, pltpu.VMEM)


VM = pl.BlockSpec(memory_space=pltpu.VMEM)
SM = pl.BlockSpec(memory_space=pltpu.SMEM)


def kernel_call(body, outs, args, scratch=(), aliases=None, flops=0, limit=8, after=(), final=False):
    count = len(args)

    def run(*refs):
        body(*refs[:count], *refs[count + len(after) :])

    place = jax.ShapeDtypeStruct if final else pltpu.VMEM
    return pl.pallas_call(
        run,
        out_shape=tuple(place(s, d) for s, d in outs),
        in_specs=[SM if a.ndim == 1 else VM for a in args] + [pl.BlockSpec(memory_space=pl.ANY)] * len(after),
        out_specs=tuple(SM if len(s) == 1 else VM for s, _ in outs),
        scratch_shapes=list(scratch),
        input_output_aliases=aliases or {},
        compiler_params=pltpu.CompilerParams(vmem_limit_bytes=limit * MIB),
        cost_estimate=pl.CostEstimate(flops=flops, bytes_accessed=0, transcendentals=0),
    )(*[a if a.ndim == 1 else vmem(a) for a in args], *after)


def encode(value, code_ref, rows):
    top = jnp.max(jnp.abs(value), axis=1, keepdims=True)
    power = jnp.floor(jnp.log2(jnp.maximum(top, 1e-30))) - 13.0
    code = jnp.round(value * jnp.exp2(-power)).astype(jnp.int32)
    code_ref[rows, :WIDTH] = code.astype(jnp.int16)
    code_ref[rows, WIDTH:] = jnp.broadcast_to(
        power.astype(jnp.int32), (value.shape[0], 128)
    ).astype(jnp.int16)


def decode(code_ref, rows):
    power = code_ref[rows, WIDTH:].astype(jnp.int32).astype(jnp.float32)[:, :1]
    return code_ref[rows, :WIDTH].astype(jnp.int32).astype(jnp.float32) * jnp.exp2(power)


def pair_terms(logits, positive):
    signed = logits if positive is None else jnp.where(positive, -logits, logits)
    small = jnp.exp(-jnp.abs(signed))
    whole = 1.0 + small
    weight = jnp.where(signed >= 0, 1.0, small) / whole
    series = small * (1.0 - small * (0.5 - small * (1.0 / 3.0)))
    loss = jnp.maximum(signed, 0.0) + jnp.where(small < 0.01, series, jnp.log(whole))
    if positive is not None:
        weight = jnp.where(positive, -weight, weight)
    return loss, weight.astype(jnp.bfloat16)


def weigh(text, image_ref, out_ref, base, groups, scale, bias, labels, scores):
    rows = text.shape[0]
    total = jnp.zeros((8, 256), jnp.float32)
    for group in groups:
        columns = slice(group * 256, group * 256 + 256)
        scores[:rows] = lax.dot_general(
            text, image_ref[columns, :], (((1,), (1,)), ((), ())), preferred_element_type=jnp.float32
        )
        for start in range(0, rows, 64):
            logits = scale * scores[start : start + 64] + bias
            positive = None
            if labels is not None and group == 0 and start < ROWS:
                row = start + lax.broadcasted_iota(jnp.int32, (64, 256), 0)
                positive = row == jnp.concatenate([labels, jnp.full_like(labels, -1)], axis=1)
            loss, weight = pair_terms(logits, positive)
            out_ref[base + start : base + start + 64, columns] = weight
            total = total + jnp.sum(loss.reshape(8, 8, 256), axis=0)
    return total[:, :128] + total[:, 128:]


def stack_body(one, two, out):
    out[:ROWS, :] = one[...]
    out[ROWS:, :] = two[...]


def choose(flag, even, odd, out):
    @pl.when(flag[0] == 0)
    def _():
        out[...] = even[...]

    @pl.when(flag[0] != 0)
    def _():
        out[...] = odd[...]


def third_body(even, odd, even_out, odd_out):
    even_out[...] = even[HALF:, :]
    odd_out[...] = odd[:HALF, :]


def early_body(scale, bias, labels, *refs):
    images, texts = refs[:4], refs[4:9]
    weights, image_all, text_all, loss, scores = refs[9:]
    for i, ref in enumerate(images):
        image_all[i * 2 * ROWS : (i + 1) * 2 * ROWS, :] = ref[...]
    for i, ref in enumerate(texts):
        text_all[i * ROWS : i * ROWS + ROWS, :] = ref[...]
    loss[...] = weigh(
        text_all[:EARLY, :], image_all, weights, 0, range(4), scale[0], bias[0], labels[...], scores
    )


def middle_body(scale, bias, even, odd, across, loss_in, weights_in, image_in, text_in, weights, image_all, text_all, loss, scores):
    del weights_in, image_in, text_in
    text_all[EARLY : EARLY + ROWS, :] = even[...]
    text_all[EARLY + ROWS : LATE, :] = odd[...]
    image_all[8 * ROWS :, :] = across[...]
    loss[...] = (
        loss_in[...]
        + weigh(
            text_all[EARLY:LATE, :], image_all, weights, EARLY, range(4), scale[0], bias[0], None, scores
        )
        + weigh(text_all[:LATE, :], image_all, weights, 0, (4,), scale[0], bias[0], None, scores)
    )


def late_body(scale, bias, first, second, image_all, loss_in, weights_in, text_in, weights, text_all, loss, code_even, code_odd, far, scores):
    del weights_in, text_in
    text_all[LATE : LATE + HALF, :] = first[...]
    text_all[LATE + HALF :, :] = second[...]
    loss[...] = loss_in[...] + weigh(
        text_all[LATE:, :], image_all, weights, LATE, range(GROUPS), scale[0], bias[0], None, scores
    )
    grad = jnp.dot(weights[EARLY:, :], image_all[...], preferred_element_type=jnp.float32)
    far[...] = grad[: 2 * ROWS]
    encode(grad[2 * ROWS : 2 * ROWS + HALF], code_even, TOP)
    encode(grad[:HALF], code_even, BOTTOM)
    encode(grad[2 * ROWS + HALF :], code_odd, TOP)
    encode(grad[ROWS + HALF : 2 * ROWS], code_odd, BOTTOM)


def text_grad_body(weights, image_all, out):
    out[...] = jnp.dot(
        weights[:EARLY, :], image_all[...], preferred_element_type=jnp.float32
    )


def hop_body(top, bottom, top_part, bottom_part, code, out):
    encode(top_part[top : top + HALF, :] + decode(code, TOP), out, TOP)
    if out.shape[0] > HALF:
        encode(bottom_part[bottom : bottom + HALF, :] + decode(code, BOTTOM), out, BOTTOM)


def text_final_body(scale, part, third_even, third_odd, fourth_even, fourth_odd, out):
    out[:HALF, :] = scale[0] * (
        part[:HALF, :] + decode(third_even, BOTTOM) + decode(fourth_odd, TOP)
    )
    out[HALF:, :] = scale[0] * (
        part[HALF:ROWS, :] + decode(third_odd, BOTTOM) + decode(fourth_even, TOP)
    )


def loss_final_body(one, two, out):
    count = float(N_LOOP * N_INNER * ROWS) * float(GROUPS * N_INNER * ROWS)
    out[0] = jnp.sum(one[...] + two[...]) / count


def loss_add_body(one, two, out):
    out[...] = one[...] + two[...]


def image_grad(weights, text_all, group):
    return lax.dot_general(
        weights[:, group * 256 : group * 256 + 256],
        text_all[...],
        (((0,), (0,)), ((), ())),
        preferred_element_type=jnp.float32,
    )


def image_code_body(weights, text_all, *outs):
    for i, group in enumerate((1, 4)):
        grad = image_grad(weights, text_all, group)
        for slot in range(2):
            encode(grad[slot * ROWS : slot * ROWS + ROWS], outs[slot], slice(i * ROWS, i * ROWS + ROWS))


def image_keep_body(weights, text_all, own, even, odd):
    for group, ref in ((0, own), (2, even), (3, odd)):
        ref[...] = image_grad(weights, text_all, group)


def chip_body(slot, flag, even, odd, code, even_out, odd_out):
    rows = slice(slot * ROWS, slot * ROWS + ROWS)
    extra = decode(code, slice(ROWS, 2 * ROWS))
    first = (flag[0] == 0).astype(jnp.float32)
    encode(even[rows, :] + first * extra, even_out, slice(0, ROWS))
    encode(odd[rows, :] + (1.0 - first) * extra, odd_out, slice(0, ROWS))


def side_body(own, other, one, two, out):
    rows = slice(0, ROWS)
    encode(
        own[ROWS:, :] + decode(other, rows) + decode(one, rows) + decode(two, rows), out, rows
    )


def image_final_body(scale, own, other, one, two, side, out):
    rows = slice(0, ROWS)
    out[...] = scale[0] * (
        own[:ROWS, :]
        + decode(other, rows)
        + decode(one, rows)
        + decode(two, rows)
        + decode(side, rows)
    )


CODE = ((HALF, CODE_WIDTH), jnp.int16)
CODE2 = ((ROWS, CODE_WIDTH), jnp.int16)
CODE4 = ((2 * ROWS, CODE_WIDTH), jnp.int16)
BF, F32 = jnp.bfloat16, jnp.float32
UNIT_FLOPS = 2 * ROWS * ROWS * WIDTH


def on_device(images, texts, labels, scale, bias):
    loop = lax.axis_index("loop")
    flag = lax.rem(loop + lax.div(loop, 2), 2).reshape(1)
    pair = ((2 * ROWS, WIDTH), BF)
    even_1, odd_1 = send(texts, Z_EVEN), send(texts, Z_ODD)
    own = kernel_call(stack_body, [pair], [images, send(images, SIDE)], after=[even_1, odd_1])[0]
    chip_even, chip_odd = send(own, CHIP_EVEN), send(own, CHIP_ODD)
    even_2, odd_2 = send(odd_1, Z_EVEN), send(even_1, Z_ODD)
    other = send(own, CORE)
    even_3, odd_3 = send(odd_2, Z_EVEN), send(even_2, Z_ODD)
    across = send(
        kernel_call(choose, [pair], [flag, chip_even, chip_odd], after=[even_3, odd_3])[0], CORE
    )
    weights, image_all, text_all, loss = kernel_call(
        early_body,
        [((TEXTS, IMAGES), BF), ((IMAGES, WIDTH), BF), ((TEXTS, WIDTH), BF), ((8, 128), F32)],
        [scale, bias, labels.reshape(1, ROWS), own, other, chip_even, chip_odd]
        + [texts, even_1, odd_1, even_2, odd_2],
        scratch=[pltpu.VMEM((EARLY, 256), F32)],
        flops=40 * UNIT_FLOPS,
        limit=16,
    )
    last_even, last_odd = kernel_call(third_body, [((HALF, WIDTH), BF)] * 2, [even_3, odd_3])
    even_4, odd_4 = send(last_odd, Z_EVEN), send(last_even, Z_ODD)
    weights, image_all, text_all, loss = kernel_call(
        middle_body,
        [((TEXTS, IMAGES), BF), ((IMAGES, WIDTH), BF), ((TEXTS, WIDTH), BF), ((8, 128), F32)],
        [scale, bias, even_3, odd_3, across, loss, weights, image_all, text_all],
        scratch=[pltpu.VMEM((LATE, 256), F32)],
        aliases={6: 0, 7: 1, 8: 2},
        flops=30 * UNIT_FLOPS,
        limit=16,
    )
    weights, text_all, loss, code_even, code_odd, far = kernel_call(
        late_body,
        [((TEXTS, IMAGES), BF), ((TEXTS, WIDTH), BF), ((8, 128), F32), CODE2, CODE2, ((2 * ROWS, WIDTH), F32)],
        [scale, bias, even_4, odd_4, image_all, loss, weights, text_all],
        scratch=[pltpu.VMEM((ROWS, 256), F32)],
        aliases={6: 0, 7: 1},
        flops=40 * UNIT_FLOPS,
        limit=16,
    )
    def add_loss(loss, route, mark):
        return kernel_call(
            loss_add_body, [((8, 128), F32)], [loss, send(loss, route)], after=[mark]
        )[0]

    even_1, odd_1 = send(code_even, Z_EVEN), send(code_odd, Z_ODD)
    codes = kernel_call(
        image_code_body, [CODE4] * 2, [weights, text_all], flops=8 * UNIT_FLOPS, limit=16,
        after=[code_even],
    )
    crossed = [send(code, CORE) for code in codes]
    near = kernel_call(
        text_grad_body, [((EARLY, WIDTH), F32)], [weights, image_all], flops=10 * UNIT_FLOPS, limit=16,
        after=[codes[0]],
    )[0]
    loss = add_loss(loss, CHIP_EVEN, near)
    keep = kernel_call(
        image_keep_body,
        [((256, WIDTH), F32)] * 3,
        [weights, text_all],
        flops=10 * UNIT_FLOPS,
        limit=16,
        after=[loss, near],
    )

    def hop(way, step, code, out=CODE2, after=()):
        half = HALF * ((step + way) % 2)
        parts = []
        for at in (step, step - 1):
            if at == 3:
                parts.append((far, way * ROWS + half))
            else:
                parts.append((near, max(2 * at - 1 + way, 0) * ROWS + half))
        (one, top), (two, bottom) = parts
        return kernel_call(
            functools.partial(hop_body, top, bottom), [out], [one, two, code], after=after,
            flops=60 * UNIT_FLOPS,
        )[0]

    def chip(slot):
        to_even, to_odd = kernel_call(
            functools.partial(chip_body, slot), [CODE2] * 2, [flag, keep[1], keep[2], crossed[slot]]
        )
        return [send(to_even, CHIP_EVEN), send(to_odd, CHIP_ODD)], to_odd

    to_even, to_odd = hop(0, 3, odd_1, after=[loss]), hop(1, 3, even_1, after=[loss])
    even_2, odd_2 = send(to_even, Z_EVEN), send(to_odd, Z_ODD)
    loss = add_loss(loss, Z_EVEN, to_odd)
    returned = [None, None]
    returned[1], mark = chip(1)
    returned[0], mark = chip(0)
    loss = add_loss(loss, ROW_FLIP, mark)
    loss = add_loss(loss, FAR_FLIP, mark)
    to_even, to_odd = hop(0, 2, odd_2, after=[loss]), hop(1, 2, even_2, after=[loss])
    even_3, odd_3 = send(to_even, Z_EVEN), send(to_odd, Z_ODD)
    loss = add_loss(loss, Z_FLIP_2, to_odd)
    to_side = kernel_call(side_body, [CODE2], [keep[0], crossed[1], *returned[1]])[0]
    from_side = send(to_side, SIDE)
    loss = add_loss(loss, CORE, to_odd)
    loss = add_loss(loss, SIDE, to_odd)
    to_even, to_odd = hop(0, 1, odd_3, CODE, after=[loss]), hop(1, 1, even_3, CODE, after=[loss])
    even_4, odd_4 = send(to_even, Z_EVEN), send(to_odd, Z_ODD)
    last = send(loss, Z_FLIP_4)
    grad_images = kernel_call(
        image_final_body,
        [((ROWS, WIDTH), F32)],
        [scale, keep[0], crossed[0], *returned[0], from_side],
        final=True,
    )[0]
    loss = kernel_call(loss_final_body, [((1,), F32)], [loss, last], final=True, after=[to_odd])[0]
    grad_texts = kernel_call(
        text_final_body,
        [((ROWS, WIDTH), F32)],
        [scale, near, even_3, odd_3, even_4, odd_4],
        final=True,
    )[0]
    return loss, grad_images, grad_texts


def solution(mesh):
    rows = P(AXES, None)
    return jax.shard_map(
        on_device,
        mesh=mesh,
        in_specs=(rows, rows, P(AXES), P(), P()),
        out_specs=(P(), rows, rows),
        check_vma=False,
    )
```

```python
import functools
import jax
import jax.numpy as jnp
from jax import lax
from jax.experimental import pallas as pl
from jax.experimental.pallas import tpu as pltpu
from jax.sharding import PartitionSpec as P

AXES = ("loop", "inner")
N_LOOP, N_INNER = 16, 16
N_Z = 8
ROWS = 128
HALF = 64
WIDTH = 1536
CODE_WIDTH = WIDTH + 128
GROUPS = 5
IMAGES = GROUPS * 2 * ROWS
TEXTS = N_Z * ROWS
NEAR = 3 * ROWS
EARLY = 5 * ROWS
LATE = 7 * ROWS
TOP = slice(0, HALF)
BOTTOM = slice(HALF, ROWS)
MIB = 1024 * 1024


def pairs(move):
    out = []
    for loop in range(N_LOOP):
        for inner in range(N_INNER):
            chip, core, z, side = loop // 2, loop % 2, inner // 2, inner % 2
            to_chip, to_core, to_z, to_side = move(chip, core, z, side)
            out.append(
                (
                    loop * N_INNER + inner,
                    ((to_chip % 8) * 2 + to_core) * N_INNER + (to_z % N_Z) * 2 + to_side,
                )
            )
    return out


def across_edge(index, first):
    return index + 1 if index % 2 == first else index - 1


Z_EVEN = pairs(lambda c, k, z, s: (c, k, across_edge(z, 0), s))
Z_ODD = pairs(lambda c, k, z, s: (c, k, across_edge(z, 1), s))
CHIP_EVEN = pairs(lambda c, k, z, s: (across_edge(c, 0), k, z, s))
CHIP_ODD = pairs(lambda c, k, z, s: (across_edge(c, 1), k, z, 1 - s if c % 4 in (0, 3) else s))
SIDE = pairs(lambda c, k, z, s: (c, k, z, 1 - s))
CORE = pairs(lambda c, k, z, s: (c, 1 - k, z, s))
def send(array, route):
    return lax.ppermute(array, AXES, route)


Z_FLIP_4 = pairs(lambda c, k, z, s: (c, k, z ^ 4, s))


def exchange(parts, axis):
    parts = parts.reshape(N_LOOP, 8, 128)
    return lax.all_to_all(parts, axis, 0, 0, tiled=True).reshape(8 * N_LOOP, 128)


def vmem(array):
    return pltpu.with_memory_space_constraint(array, pltpu.VMEM)


VM = pl.BlockSpec(memory_space=pltpu.VMEM)
SM = pl.BlockSpec(memory_space=pltpu.SMEM)


def kernel_call(body, outs, args, scratch=(), aliases=None, flops=0, limit=8, after=(), final=False):
    count = len(args)

    def run(*refs):
        body(*refs[:count], *refs[count + len(after) :])

    place = jax.ShapeDtypeStruct if final else pltpu.VMEM
    return pl.pallas_call(
        run,
        out_shape=tuple(place(s, d) for s, d in outs),
        in_specs=[SM if a.ndim == 1 else VM for a in args] + [pl.BlockSpec(memory_space=pl.ANY)] * len(after),
        out_specs=tuple(SM if len(s) == 1 else VM for s, _ in outs),
        scratch_shapes=list(scratch),
        input_output_aliases=aliases or {},
        compiler_params=pltpu.CompilerParams(vmem_limit_bytes=limit * MIB),
        cost_estimate=pl.CostEstimate(flops=flops, bytes_accessed=0, transcendentals=0),
    )(*[a if a.ndim == 1 or final else vmem(a) for a in args], *after)


def encode(value, code_ref, rows, digits=None):
    top = jnp.max(jnp.abs(value), axis=1, keepdims=True)
    power = jnp.floor(jnp.log2(jnp.maximum(top, 1e-30))) - 13.0
    code = jnp.round(value * jnp.exp2(-power)).astype(jnp.int32)
    code_ref[rows, :WIDTH] = code.astype(jnp.int16)
    added = jnp.broadcast_to(power.astype(jnp.int32), (value.shape[0], 128))
    if digits is not None:
        lane = lax.broadcasted_iota(jnp.int32, added.shape, 1)
        added = jnp.where(lane < 32, added, jnp.broadcast_to(digits, added.shape))
    code_ref[rows, WIDTH:] = added.astype(jnp.int16)


def to_digits(total):
    power = jnp.floor(jnp.log2(jnp.maximum(total, 1e-30))) - 13.0
    scaled = total * jnp.exp2(-power)
    high = jnp.floor(scaled)
    low = jnp.round((scaled - high) * 8192.0)
    lane = lax.broadcasted_iota(jnp.int32, total.shape, 1)
    return jnp.where(lane < 64, power, jnp.where(lane < 96, high, low)).astype(jnp.int32)


def read_digits(code_ref):
    return code_ref[:16, WIDTH:].astype(jnp.int32)[:1, :]


def from_digits(digits):
    power, high, low = (digits[:, at : at + 1].astype(jnp.float32) for at in (32, 64, 96))
    return (high + low * (1.0 / 8192.0)) * jnp.exp2(power)


def decode(code_ref, rows):
    power = code_ref[rows, WIDTH:].astype(jnp.int32).astype(jnp.float32)[:, :1]
    return code_ref[rows, :WIDTH].astype(jnp.int32).astype(jnp.float32) * jnp.exp2(power)


def pair_terms(logits, positive):
    signed = logits if positive is None else jnp.where(positive, -logits, logits)
    small = jnp.exp(-jnp.abs(signed))
    whole = 1.0 + small
    weight = jnp.where(signed >= 0, 1.0, small) / whole
    series = small * (1.0 - small * (0.5 - small * (1.0 / 3.0)))
    loss = jnp.maximum(signed, 0.0) + jnp.where(small < 0.01, series, jnp.log(whole))
    if positive is not None:
        weight = jnp.where(positive, -weight, weight)
    return loss, weight.astype(jnp.bfloat16)


def weigh(text, image_ref, out_ref, base, groups, scale, bias, labels, scores):
    rows = text.shape[0]
    total = jnp.zeros((8, 256), jnp.float32)
    for group in groups:
        columns = slice(group * 256, group * 256 + 256)
        scores[:rows] = lax.dot_general(
            text, image_ref[columns, :], (((1,), (1,)), ((), ())), preferred_element_type=jnp.float32
        )
        for start in range(0, rows, 64):
            logits = scale * scores[start : start + 64] + bias
            positive = None
            if labels is not None and group == 0 and start < ROWS:
                row = start + lax.broadcasted_iota(jnp.int32, (64, 256), 0)
                positive = row == jnp.concatenate([labels, jnp.full_like(labels, -1)], axis=1)
            loss, weight = pair_terms(logits, positive)
            out_ref[base + start : base + start + 64, columns] = weight
            total = total + jnp.sum(loss.reshape(8, 8, 256), axis=0)
    return total[:, :128] + total[:, 128:]


def pass_body(array, out):
    del array, out


def choose_body(place, even0, even1, odd0, odd1, out):
    @pl.when(lax.rem(place[0], 2) == 0)
    def _():
        out[:ROWS, :] = even0[...]
        out[ROWS:, :] = even1[...]

    @pl.when(lax.rem(place[0], 2) != 0)
    def _():
        out[:ROWS, :] = odd0[...]
        out[ROWS:, :] = odd1[...]


def third_body(even, odd, even_out, odd_out):
    even_out[...] = even[HALF:, :]
    odd_out[...] = odd[:HALF, :]


def early_body(scale, bias, labels, *refs):
    images, texts = refs[:8], refs[8:13]
    weights, image_all, text_all, loss, scores = refs[13:]
    for i, ref in enumerate(images):
        image_all[i * ROWS : i * ROWS + ROWS, :] = ref[...]
    for i, ref in enumerate(texts):
        text_all[i * ROWS : i * ROWS + ROWS, :] = ref[...]
    loss[...] = weigh(
        text_all[:EARLY, :], image_all, weights, 0, range(4), scale[0], bias[0], labels[...], scores
    )


def middle_body(scale, bias, even, odd, across, loss_in, weights_in, image_in, text_in, weights, image_all, text_all, loss, scores):
    del weights_in, image_in, text_in
    text_all[EARLY : EARLY + ROWS, :] = even[...]
    text_all[EARLY + ROWS : LATE, :] = odd[...]
    image_all[8 * ROWS :, :] = across[...]
    loss[...] = (
        loss_in[...]
        + weigh(
            text_all[EARLY:LATE, :], image_all, weights, EARLY, range(4), scale[0], bias[0], None, scores
        )
        + weigh(text_all[:LATE, :], image_all, weights, 0, (4,), scale[0], bias[0], None, scores)
    )


def late_body(scale, bias, first, second, image_all, loss_in, weights_in, text_in, weights, text_all, loss, code_even, code_odd, far, scores):
    del weights_in, text_in
    text_all[LATE : LATE + HALF, :] = first[...]
    text_all[LATE + HALF :, :] = second[...]
    total = jnp.sum(
        loss_in[...]
        + weigh(
            text_all[LATE:, :], image_all, weights, LATE, range(GROUPS), scale[0], bias[0], None, scores
        )
    )
    digits = to_digits(jnp.full((1, 128), total, jnp.float32))
    loss[...] = jnp.broadcast_to(from_digits(digits), (8, 128))
    grad = jnp.dot(weights[NEAR:, :], image_all[...], preferred_element_type=jnp.float32)
    far[...] = grad[: 4 * ROWS]
    encode(grad[4 * ROWS : 4 * ROWS + HALF], code_even, TOP, digits)
    encode(grad[2 * ROWS : 2 * ROWS + HALF], code_even, BOTTOM, digits)
    encode(grad[4 * ROWS + HALF :], code_odd, TOP, digits)
    encode(grad[3 * ROWS + HALF : 4 * ROWS], code_odd, BOTTOM, digits)


def text_grad_body(weights, image_all, out):
    out[...] = jnp.dot(
        weights[:NEAR, :], image_all[...], preferred_element_type=jnp.float32
    )


def hop_body(top, bottom, top_part, bottom_part, code, out):
    digits = read_digits(code)
    encode(top_part[top : top + HALF, :] + decode(code, TOP), out, TOP, digits)
    if out.shape[0] > HALF:
        encode(bottom_part[bottom : bottom + HALF, :] + decode(code, BOTTOM), out, BOTTOM, digits)


def text_final_body(scale, part, third_even, third_odd, fourth_even, fourth_odd, out, done):
    done[...] = jnp.zeros((8, 128), jnp.float32)
    out[:HALF, :] = scale[0] * (
        part[:HALF, :] + decode(third_even, BOTTOM) + decode(fourth_odd, TOP)
    )
    out[HALF:, :] = scale[0] * (
        part[HALF:ROWS, :] + decode(third_odd, BOTTOM) + decode(fourth_even, TOP)
    )


def loss_sum(parts):
    total = parts[:8, :]
    for start in range(8, 8 * N_LOOP, 8):
        total = total + parts[start : start + 8, :]
    return total


def loss_ring_body(place, own, opposite, *refs):
    *codes, out = refs
    lane = lax.broadcasted_iota(jnp.int32, (8, 128), 1)
    z = lax.div(place[0], 2)
    step = 1 - 2 * lax.rem(z, 2)
    total = jnp.where(lane == z, own[...], 0.0)
    total = total + jnp.where(lane == lax.rem(z + 4, N_Z), opposite[...], 0.0)
    for i, code in enumerate(codes):
        distance = (i // 2 + 1) * (1 - 2 * (i % 2))
        other = lax.rem(z + step * distance + N_Z, N_Z)
        value = jnp.broadcast_to(from_digits(read_digits(code)), (8, 128))
        total = total + jnp.where(lane == other, value, 0.0)
    out[...] = total


def loss_side_body(one, two, out):
    total = one[...] + two[...]
    for i in range(N_LOOP):
        out[8 * i : 8 * i + 8, :] = total


def loss_final_body(parts, out):
    count = float(N_LOOP * N_INNER * ROWS) * float(GROUPS * N_INNER * ROWS)
    out[0] = jnp.sum(loss_sum(parts)[:1, :]) / count


def image_grad(weights, text_all, group):
    return lax.dot_general(
        weights[:, group * 256 : group * 256 + 256],
        text_all[...],
        (((0,), (0,)), ((), ())),
        preferred_element_type=jnp.float32,
    )


def image_code_body(weights, text_all, *outs):
    for i, group in enumerate((1, 4)):
        grad = image_grad(weights, text_all, group)
        for slot in range(2):
            encode(grad[slot * ROWS : slot * ROWS + ROWS], outs[slot], slice(i * ROWS, i * ROWS + ROWS))


def image_keep_body(weights, text_all, own, even, odd):
    for group, ref in ((0, own), (2, even), (3, odd)):
        ref[...] = image_grad(weights, text_all, group)


def chip_body(slot, place, even, odd, code, even_out, odd_out):
    rows = slice(slot * ROWS, slot * ROWS + ROWS)
    extra = decode(code, slice(ROWS, 2 * ROWS))
    first = (lax.rem(place[0], 2) == 0).astype(jnp.float32)
    encode(even[rows, :] + first * extra, even_out, slice(0, ROWS))
    encode(odd[rows, :] + (1.0 - first) * extra, odd_out, slice(0, ROWS))


def side_body(own, other, one, two, out):
    rows = slice(0, ROWS)
    encode(
        own[ROWS:, :] + decode(other, rows) + decode(one, rows) + decode(two, rows), out, rows
    )


def image_sum_body(own, other, one, two, out):
    rows = slice(0, ROWS)
    out[...] = own[:ROWS, :] + decode(other, rows) + decode(one, rows) + decode(two, rows)


def image_final_body(scale, part, side, out, done):
    done[...] = jnp.zeros((8, 128), jnp.float32)
    out[...] = scale[0] * (part[...] + decode(side, slice(0, ROWS)))


CODE = ((HALF, CODE_WIDTH), jnp.int16)
CODE2 = ((ROWS, CODE_WIDTH), jnp.int16)
CODE4 = ((2 * ROWS, CODE_WIDTH), jnp.int16)
BF, F32 = jnp.bfloat16, jnp.float32
UNIT_FLOPS = 2 * ROWS * ROWS * WIDTH
LOSSES = ((8 * N_LOOP, 128), F32)


def on_device(images, texts, labels, scale, bias):
    loop = lax.axis_index("loop")
    place = (
        2 * lax.div(lax.axis_index("inner"), 2) + lax.rem(loop + lax.div(loop, 2), 2)
    ).reshape(1)
    even_1, odd_1 = send(texts, Z_EVEN), send(texts, Z_ODD)
    own = [images, send(images, SIDE)]
    chip_even, chip_odd = [send(images, CHIP_EVEN)], [send(images, CHIP_ODD)]
    own[1] = kernel_call(
        pass_body, [((ROWS, WIDTH), BF)], [own[1]], aliases={0: 0}, after=[chip_even[0], chip_odd[0]]
    )[0]
    chip_even.append(send(own[1], CHIP_EVEN))
    chip_odd.append(send(own[1], CHIP_ODD))
    even_2, odd_2 = send(odd_1, Z_EVEN), send(even_1, Z_ODD)
    other = [send(a, CORE) for a in own]
    even_3, odd_3 = send(odd_2, Z_EVEN), send(even_2, Z_ODD)
    across = send(
        kernel_call(choose_body, [((2 * ROWS, WIDTH), BF)], [place, *chip_even, *chip_odd])[0], CORE
    )
    weights, image_all, text_all, loss = kernel_call(
        early_body,
        [((TEXTS, IMAGES), BF), ((IMAGES, WIDTH), BF), ((TEXTS, WIDTH), BF), ((8, 128), F32)],
        [scale, bias, labels.reshape(1, ROWS), *own, *other, *chip_even, *chip_odd]
        + [texts, even_1, odd_1, even_2, odd_2],
        scratch=[pltpu.VMEM((EARLY, 256), F32)],
        flops=40 * UNIT_FLOPS,
        limit=16,
    )
    last_even, last_odd = kernel_call(
        third_body, [((HALF, WIDTH), BF)] * 2, [even_3, odd_3], flops=60 * UNIT_FLOPS, after=[loss]
    )
    even_4, odd_4 = send(last_odd, Z_EVEN), send(last_even, Z_ODD)
    weights, image_all, text_all, loss = kernel_call(
        middle_body,
        [((TEXTS, IMAGES), BF), ((IMAGES, WIDTH), BF), ((TEXTS, WIDTH), BF), ((8, 128), F32)],
        [scale, bias, even_3, odd_3, across, loss, weights, image_all, text_all],
        scratch=[pltpu.VMEM((LATE, 256), F32)],
        aliases={6: 0, 7: 1, 8: 2},
        flops=30 * UNIT_FLOPS,
        limit=16,
    )
    weights, text_all, loss, code_even, code_odd, far = kernel_call(
        late_body,
        [((TEXTS, IMAGES), BF), ((TEXTS, WIDTH), BF), ((8, 128), F32), CODE2, CODE2, ((4 * ROWS, WIDTH), F32)],
        [scale, bias, even_4, odd_4, image_all, loss, weights, text_all],
        scratch=[pltpu.VMEM((ROWS, 256), F32)],
        aliases={6: 0, 7: 1},
        flops=40 * UNIT_FLOPS,
        limit=16,
    )
    even_1, odd_1 = send(code_even, Z_EVEN), send(code_odd, Z_ODD)
    opposite = send(loss, Z_FLIP_4)
    codes = kernel_call(
        image_code_body, [CODE4] * 2, [weights, text_all], flops=8 * UNIT_FLOPS, limit=16,
        after=[code_even],
    )
    crossed = [send(code, CORE) for code in codes]
    keep = kernel_call(
        image_keep_body,
        [((256, WIDTH), F32)] * 3,
        [weights, text_all],
        flops=10 * UNIT_FLOPS,
        limit=16,
        after=[codes[0]],
    )

    def hop(way, step, code, out=CODE2, after=(), final=False):
        half = HALF * ((step + way) % 2)
        parts = []
        for at in (step, step - 1):
            if at >= 2:
                parts.append((far, (2 * at - 4 + way) * ROWS + half))
            else:
                parts.append((near, max(2 * at - 1 + way, 0) * ROWS + half))
        (one, top), (two, bottom) = parts
        return kernel_call(
            functools.partial(hop_body, top, bottom), [out], [one, two, code],
            flops=400 * UNIT_FLOPS, final=final, after=after,
        )[0]

    def chip(slot):
        to_even, to_odd = kernel_call(
            functools.partial(chip_body, slot), [CODE2] * 2, [place, keep[1], keep[2], crossed[slot]],
            flops=300 * UNIT_FLOPS,
        )
        return [send(to_even, CHIP_EVEN), send(to_odd, CHIP_ODD)], to_odd

    to_even, to_odd = hop(0, 3, odd_1), hop(1, 3, even_1)
    even_2, odd_2 = send(to_even, Z_EVEN), send(to_odd, Z_ODD)
    returned = [None, None]
    returned[1], mark = chip(1)
    near = kernel_call(
        text_grad_body, [((NEAR, WIDTH), F32)], [weights, image_all], flops=10 * UNIT_FLOPS, limit=16,
        after=[mark],
    )[0]
    returned[0], mark = chip(0)
    to_even, to_odd = hop(0, 2, odd_2), hop(1, 2, even_2)
    even_3, odd_3 = send(to_even, Z_EVEN), send(to_odd, Z_ODD)
    to_side = kernel_call(
        side_body, [CODE2], [keep[0], crossed[1], *returned[1]], final=True, flops=300 * UNIT_FLOPS
    )[0]
    from_side = send(to_side, SIDE)
    to_even, to_odd = hop(0, 1, odd_3, CODE, final=True), hop(1, 1, even_3, CODE, after=[opposite], final=True)
    even_4, odd_4 = send(to_even, Z_EVEN), send(to_odd, Z_ODD)
    image_part = kernel_call(
        image_sum_body, [((ROWS, WIDTH), F32)], [keep[0], crossed[0], *returned[0]]
    )[0]
    loss = kernel_call(
        loss_ring_body,
        [((8, 128), F32)],
        [place, loss, opposite, even_1, odd_1, even_2, odd_2, even_3, odd_3],
        after=[to_odd, image_part],
    )[0]
    grad_images, images_done = kernel_call(
        image_final_body,
        [((ROWS, WIDTH), F32), ((8, 128), F32)],
        [scale, image_part, from_side],
        final=True,
    )
    grad_texts, texts_done = kernel_call(
        text_final_body,
        [((ROWS, WIDTH), F32), ((8, 128), F32)],
        [scale, near, even_3, odd_3, even_4, odd_4],
        final=True,
    )
    parts = kernel_call(
        loss_side_body, [LOSSES], [loss, send(loss, SIDE)], final=True, after=[images_done, texts_done]
    )[0]
    parts = exchange(parts, "loop")
    loss = kernel_call(loss_final_body, [((1,), F32)], [parts], final=True)[0]
    return loss, grad_images, grad_texts


def solution(mesh):
    rows = P(AXES, None)
    return jax.shard_map(
        on_device,
        mesh=mesh,
        in_specs=(rows, rows, P(AXES), P(), P()),
        out_specs=(P(), rows, rows),
        check_vma=False,
    )
```

```python
import functools
import jax
import jax.numpy as jnp
from jax import lax
from jax.experimental import pallas as pl
from jax.experimental.pallas import tpu as pltpu
from jax.sharding import PartitionSpec as P

AXES = ("loop", "inner")
N_LOOP, N_INNER = 16, 16
N_Z = 8
ROWS = 128
HALF = 64
WIDTH = 1536
CODE_WIDTH = WIDTH + 128
GROUPS = 5
IMAGES = GROUPS * 2 * ROWS
TEXTS = N_Z * ROWS
NEAR = 3 * ROWS
EARLY = 5 * ROWS
LATE = 7 * ROWS
TOP = slice(0, HALF)
BOTTOM = slice(HALF, ROWS)
MIB = 1024 * 1024


def pairs(move):
    out = []
    for loop in range(N_LOOP):
        for inner in range(N_INNER):
            chip, core, z, side = loop // 2, loop % 2, inner // 2, inner % 2
            to_chip, to_core, to_z, to_side = move(chip, core, z, side)
            out.append(
                (
                    loop * N_INNER + inner,
                    ((to_chip % 8) * 2 + to_core) * N_INNER + (to_z % N_Z) * 2 + to_side,
                )
            )
    return out


def across_edge(index, first):
    return index + 1 if index % 2 == first else index - 1


Z_EVEN = pairs(lambda c, k, z, s: (c, k, across_edge(z, 0), s))
Z_ODD = pairs(lambda c, k, z, s: (c, k, across_edge(z, 1), s))
CHIP_EVEN = pairs(lambda c, k, z, s: (across_edge(c, 0), k, z, s))
CHIP_ODD = pairs(lambda c, k, z, s: (across_edge(c, 1), k, z, 1 - s if c % 4 in (0, 3) else s))
SIDE = pairs(lambda c, k, z, s: (c, k, z, 1 - s))
CORE = pairs(lambda c, k, z, s: (c, 1 - k, z, s))
def send(array, route):
    return lax.ppermute(array, AXES, route)


Z_FLIP_4 = pairs(lambda c, k, z, s: (c, k, z ^ 4, s))


def exchange(parts, axis):
    parts = parts.reshape(N_LOOP, 8, 128)
    return lax.all_to_all(parts, axis, 0, 0, tiled=True).reshape(8 * N_LOOP, 128)


def vmem(array):
    return pltpu.with_memory_space_constraint(array, pltpu.VMEM)


VM = pl.BlockSpec(memory_space=pltpu.VMEM)
SM = pl.BlockSpec(memory_space=pltpu.SMEM)


def kernel_call(body, outs, args, scratch=(), aliases=None, flops=0, limit=8, after=(), final=False):
    count = len(args)

    def run(*refs):
        body(*refs[:count], *refs[count + len(after) :])

    place = jax.ShapeDtypeStruct if final else pltpu.VMEM
    return pl.pallas_call(
        run,
        out_shape=tuple(place(s, d) for s, d in outs),
        in_specs=[SM if a.ndim == 1 else VM for a in args] + [pl.BlockSpec(memory_space=pl.ANY)] * len(after),
        out_specs=tuple(SM if len(s) == 1 else VM for s, _ in outs),
        scratch_shapes=list(scratch),
        input_output_aliases=aliases or {},
        compiler_params=pltpu.CompilerParams(vmem_limit_bytes=limit * MIB),
        cost_estimate=pl.CostEstimate(flops=flops, bytes_accessed=0, transcendentals=0),
    )(*[a if a.ndim == 1 or final else vmem(a) for a in args], *after)


def encode(value, code_ref, rows, digits=None):
    top = jnp.max(jnp.abs(value), axis=1, keepdims=True)
    power = jnp.floor(jnp.log2(jnp.maximum(top, 1e-30))) - 13.0
    code = jnp.round(value * jnp.exp2(-power)).astype(jnp.int32)
    code_ref[rows, :WIDTH] = code.astype(jnp.int16)
    added = jnp.broadcast_to(power.astype(jnp.int32), (value.shape[0], 128))
    if digits is not None:
        lane = lax.broadcasted_iota(jnp.int32, added.shape, 1)
        added = jnp.where(lane < 32, added, jnp.broadcast_to(digits, added.shape))
    code_ref[rows, WIDTH:] = added.astype(jnp.int16)


def to_digits(total):
    power = jnp.floor(jnp.log2(jnp.maximum(total, 1e-30))) - 13.0
    scaled = total * jnp.exp2(-power)
    high = jnp.floor(scaled)
    low = jnp.round((scaled - high) * 8192.0)
    lane = lax.broadcasted_iota(jnp.int32, total.shape, 1)
    return jnp.where(lane < 64, power, jnp.where(lane < 96, high, low)).astype(jnp.int32)


def read_digits(code_ref):
    return code_ref[:16, WIDTH:].astype(jnp.int32)[:1, :]


def from_digits(digits):
    power, high, low = (digits[:, at : at + 1].astype(jnp.float32) for at in (32, 64, 96))
    return (high + low * (1.0 / 8192.0)) * jnp.exp2(power)


def decode(code_ref, rows):
    power = code_ref[rows, WIDTH:].astype(jnp.int32).astype(jnp.float32)[:, :1]
    return code_ref[rows, :WIDTH].astype(jnp.int32).astype(jnp.float32) * jnp.exp2(power)


def pair_terms(logits, positive):
    signed = logits if positive is None else jnp.where(positive, -logits, logits)
    small = jnp.exp(-jnp.abs(signed))
    whole = 1.0 + small
    weight = jnp.where(signed >= 0, 1.0, small) / whole
    series = small * (1.0 - small * (0.5 - small * (1.0 / 3.0)))
    loss = jnp.maximum(signed, 0.0) + jnp.where(small < 0.01, series, jnp.log(whole))
    if positive is not None:
        weight = jnp.where(positive, -weight, weight)
    return loss, weight.astype(jnp.bfloat16)


def weigh(text, image_ref, out_ref, base, groups, scale, bias, labels, scores):
    rows = text.shape[0]
    total = jnp.zeros((8, 256), jnp.float32)
    for group in groups:
        columns = slice(group * 256, group * 256 + 256)
        scores[:rows] = lax.dot_general(
            text, image_ref[columns, :], (((1,), (1,)), ((), ())), preferred_element_type=jnp.float32
        )
        for start in range(0, rows, 64):
            logits = scale * scores[start : start + 64] + bias
            positive = None
            if labels is not None and group == 0 and start < ROWS:
                row = start + lax.broadcasted_iota(jnp.int32, (64, 256), 0)
                positive = row == jnp.concatenate([labels, jnp.full_like(labels, -1)], axis=1)
            loss, weight = pair_terms(logits, positive)
            out_ref[base + start : base + start + 64, columns] = weight
            total = total + jnp.sum(loss.reshape(8, 8, 256), axis=0)
    return total[:, :128] + total[:, 128:]


def pass_body(array, out):
    del array, out


def choose_body(place, even0, even1, odd0, odd1, out):
    @pl.when(lax.rem(place[0], 2) == 0)
    def _():
        out[:ROWS, :] = even0[...]
        out[ROWS:, :] = even1[...]

    @pl.when(lax.rem(place[0], 2) != 0)
    def _():
        out[:ROWS, :] = odd0[...]
        out[ROWS:, :] = odd1[...]


def third_body(even, odd, even_out, odd_out):
    even_out[...] = even[HALF:, :]
    odd_out[...] = odd[:HALF, :]


def early_body(scale, bias, labels, *refs):
    images, texts = refs[:8], refs[8:13]
    weights, image_all, text_all, loss, scores = refs[13:]
    for i, ref in enumerate(images):
        image_all[i * ROWS : i * ROWS + ROWS, :] = ref[...]
    for i, ref in enumerate(texts):
        text_all[i * ROWS : i * ROWS + ROWS, :] = ref[...]
    loss[...] = weigh(
        text_all[:EARLY, :], image_all, weights, 0, range(4), scale[0], bias[0], labels[...], scores
    )


def middle_body(scale, bias, even, odd, across, loss_in, weights_in, image_in, text_in, weights, image_all, text_all, loss, scores):
    del weights_in, image_in, text_in
    text_all[EARLY : EARLY + ROWS, :] = even[...]
    text_all[EARLY + ROWS : LATE, :] = odd[...]
    image_all[8 * ROWS :, :] = across[...]
    loss[...] = (
        loss_in[...]
        + weigh(
            text_all[EARLY:LATE, :], image_all, weights, EARLY, range(4), scale[0], bias[0], None, scores
        )
        + weigh(text_all[:LATE, :], image_all, weights, 0, (4,), scale[0], bias[0], None, scores)
    )


def late_body(scale, bias, first, second, image_all, loss_in, weights_in, text_in, weights, text_all, loss, code_even, code_odd, far, scores):
    del weights_in, text_in
    text_all[LATE : LATE + HALF, :] = first[...]
    text_all[LATE + HALF :, :] = second[...]
    total = jnp.sum(
        loss_in[...]
        + weigh(
            text_all[LATE:, :], image_all, weights, LATE, range(GROUPS), scale[0], bias[0], None, scores
        )
    )
    digits = to_digits(jnp.full((1, 128), total, jnp.float32))
    loss[...] = jnp.broadcast_to(from_digits(digits), (8, 128))
    grad = jnp.dot(weights[NEAR:, :], image_all[...], preferred_element_type=jnp.float32)
    far[...] = grad[: 4 * ROWS]
    encode(grad[4 * ROWS : 4 * ROWS + HALF], code_even, TOP, digits)
    encode(grad[2 * ROWS : 2 * ROWS + HALF], code_even, BOTTOM, digits)
    encode(grad[4 * ROWS + HALF :], code_odd, TOP, digits)
    encode(grad[3 * ROWS + HALF : 4 * ROWS], code_odd, BOTTOM, digits)


def text_grad_body(weights, image_all, out):
    out[...] = jnp.dot(
        weights[:NEAR, :], image_all[...], preferred_element_type=jnp.float32
    )


def hop_body(top, bottom, top_part, bottom_part, code, out):
    digits = read_digits(code)
    encode(top_part[top : top + HALF, :] + decode(code, TOP), out, TOP, digits)
    if out.shape[0] > HALF:
        encode(bottom_part[bottom : bottom + HALF, :] + decode(code, BOTTOM), out, BOTTOM, digits)


def text_final_body(scale, part, third_even, third_odd, fourth_even, fourth_odd, out, done):
    done[...] = jnp.zeros((8, 128), jnp.float32)
    out[:HALF, :] = scale[0] * (
        part[:HALF, :] + decode(third_even, BOTTOM) + decode(fourth_odd, TOP)
    )
    out[HALF:, :] = scale[0] * (
        part[HALF:ROWS, :] + decode(third_odd, BOTTOM) + decode(fourth_even, TOP)
    )


def loss_sum(parts):
    total = parts[:8, :]
    for start in range(8, 8 * N_LOOP, 8):
        total = total + parts[start : start + 8, :]
    return total


def loss_ring_body(place, own, opposite, *refs):
    *codes, out = refs
    lane = lax.broadcasted_iota(jnp.int32, (8, 128), 1)
    z = lax.div(place[0], 2)
    step = 1 - 2 * lax.rem(z, 2)
    total = jnp.where(lane == z, own[...], 0.0)
    total = total + jnp.where(lane == lax.rem(z + 4, N_Z), opposite[...], 0.0)
    for i, code in enumerate(codes):
        distance = (i // 2 + 1) * (1 - 2 * (i % 2))
        other = lax.rem(z + step * distance + N_Z, N_Z)
        value = jnp.broadcast_to(from_digits(read_digits(code)), (8, 128))
        total = total + jnp.where(lane == other, value, 0.0)
    out[...] = total


def loss_side_body(one, two, out):
    total = one[...] + two[...]
    for i in range(N_LOOP):
        out[8 * i : 8 * i + 8, :] = total


def loss_final_body(parts, out):
    count = float(N_LOOP * N_INNER * ROWS) * float(GROUPS * N_INNER * ROWS)
    out[0] = jnp.sum(loss_sum(parts)[:1, :]) / count


def image_grad(weights, text_all, group):
    return lax.dot_general(
        weights[:, group * 256 : group * 256 + 256],
        text_all[...],
        (((0,), (0,)), ((), ())),
        preferred_element_type=jnp.float32,
    )


def image_code_body(weights, text_all, *outs):
    for i, group in enumerate((1, 4)):
        grad = image_grad(weights, text_all, group)
        for slot in range(2):
            encode(grad[slot * ROWS : slot * ROWS + ROWS], outs[slot], slice(i * ROWS, i * ROWS + ROWS))


def image_keep_body(weights, text_all, own, even, odd):
    for group, ref in ((0, own), (2, even), (3, odd)):
        ref[...] = image_grad(weights, text_all, group)


def chip_body(slot, place, even, odd, code, even_out, odd_out):
    rows = slice(slot * ROWS, slot * ROWS + ROWS)
    extra = decode(code, slice(ROWS, 2 * ROWS))
    first = (lax.rem(place[0], 2) == 0).astype(jnp.float32)
    encode(even[rows, :] + first * extra, even_out, slice(0, ROWS))
    encode(odd[rows, :] + (1.0 - first) * extra, odd_out, slice(0, ROWS))


def side_body(own, other, one, two, out):
    rows = slice(0, ROWS)
    encode(
        own[ROWS:, :] + decode(other, rows) + decode(one, rows) + decode(two, rows), out, rows
    )


def image_sum_body(own, other, one, two, out):
    rows = slice(0, ROWS)
    out[...] = own[:ROWS, :] + decode(other, rows) + decode(one, rows) + decode(two, rows)


def image_final_body(scale, part, side, out, done):
    done[...] = jnp.zeros((8, 128), jnp.float32)
    out[...] = scale[0] * (part[...] + decode(side, slice(0, ROWS)))


CODE = ((HALF, CODE_WIDTH), jnp.int16)
CODE2 = ((ROWS, CODE_WIDTH), jnp.int16)
CODE4 = ((2 * ROWS, CODE_WIDTH), jnp.int16)
BF, F32 = jnp.bfloat16, jnp.float32
UNIT_FLOPS = 2 * ROWS * ROWS * WIDTH
LOSSES = ((8 * N_LOOP, 128), F32)


def on_device(images, texts, labels, scale, bias):
    loop = lax.axis_index("loop")
    place = (
        2 * lax.div(lax.axis_index("inner"), 2) + lax.rem(loop + lax.div(loop, 2), 2)
    ).reshape(1)
    even_1, odd_1 = send(texts, Z_EVEN), send(texts, Z_ODD)
    own = [images, send(images, SIDE)]
    chip_even, chip_odd = [send(images, CHIP_EVEN)], [send(images, CHIP_ODD)]
    own[1] = kernel_call(
        pass_body, [((ROWS, WIDTH), BF)], [own[1]], aliases={0: 0}, after=[chip_even[0], chip_odd[0]]
    )[0]
    chip_even.append(send(own[1], CHIP_EVEN))
    chip_odd.append(send(own[1], CHIP_ODD))
    even_2, odd_2 = send(odd_1, Z_EVEN), send(even_1, Z_ODD)
    other = [send(a, CORE) for a in own]
    even_3, odd_3 = send(odd_2, Z_EVEN), send(even_2, Z_ODD)
    across = send(
        kernel_call(choose_body, [((2 * ROWS, WIDTH), BF)], [place, *chip_even, *chip_odd])[0], CORE
    )
    weights, image_all, text_all, loss = kernel_call(
        early_body,
        [((TEXTS, IMAGES), BF), ((IMAGES, WIDTH), BF), ((TEXTS, WIDTH), BF), ((8, 128), F32)],
        [scale, bias, labels.reshape(1, ROWS), *own, *other, *chip_even, *chip_odd]
        + [texts, even_1, odd_1, even_2, odd_2],
        scratch=[pltpu.VMEM((EARLY, 256), F32)],
        flops=40 * UNIT_FLOPS,
        limit=16,
    )
    last_even, last_odd = kernel_call(
        third_body, [((HALF, WIDTH), BF)] * 2, [even_3, odd_3], flops=60 * UNIT_FLOPS, after=[loss]
    )
    even_4, odd_4 = send(last_odd, Z_EVEN), send(last_even, Z_ODD)
    weights, image_all, text_all, loss = kernel_call(
        middle_body,
        [((TEXTS, IMAGES), BF), ((IMAGES, WIDTH), BF), ((TEXTS, WIDTH), BF), ((8, 128), F32)],
        [scale, bias, even_3, odd_3, across, loss, weights, image_all, text_all],
        scratch=[pltpu.VMEM((LATE, 256), F32)],
        aliases={6: 0, 7: 1, 8: 2},
        flops=30 * UNIT_FLOPS,
        limit=16,
    )
    weights, text_all, loss, code_even, code_odd, far = kernel_call(
        late_body,
        [((TEXTS, IMAGES), BF), ((TEXTS, WIDTH), BF), ((8, 128), F32), CODE2, CODE2, ((4 * ROWS, WIDTH), F32)],
        [scale, bias, even_4, odd_4, image_all, loss, weights, text_all],
        scratch=[pltpu.VMEM((ROWS, 256), F32)],
        aliases={6: 0, 7: 1},
        flops=40 * UNIT_FLOPS,
        limit=16,
    )
    even_1, odd_1 = send(code_even, Z_EVEN), send(code_odd, Z_ODD)
    opposite = send(loss, Z_FLIP_4)
    codes = kernel_call(
        image_code_body, [CODE4] * 2, [weights, text_all], flops=8 * UNIT_FLOPS, limit=16,
        after=[code_even],
    )
    crossed = [send(code, CORE) for code in codes]
    keep = kernel_call(
        image_keep_body,
        [((256, WIDTH), F32)] * 3,
        [weights, text_all],
        flops=10 * UNIT_FLOPS,
        limit=16,
        after=[codes[0]],
    )

    def hop(way, step, code, out=CODE2, after=(), final=False):
        half = HALF * ((step + way) % 2)
        parts = []
        for at in (step, step - 1):
            if at >= 2:
                parts.append((far, (2 * at - 4 + way) * ROWS + half))
            else:
                parts.append((near, max(2 * at - 1 + way, 0) * ROWS + half))
        (one, top), (two, bottom) = parts
        return kernel_call(
            functools.partial(hop_body, top, bottom), [out], [one, two, code],
            flops=400 * UNIT_FLOPS, final=final, after=after,
        )[0]

    def chip(slot, after=()):
        to_even, to_odd = kernel_call(
            functools.partial(chip_body, slot), [CODE2] * 2, [place, keep[1], keep[2], crossed[slot]],
            flops=300 * UNIT_FLOPS, after=after,
        )
        return [send(to_even, CHIP_EVEN), send(to_odd, CHIP_ODD)], to_odd

    to_even, to_odd = hop(0, 3, odd_1), hop(1, 3, even_1)
    even_2, odd_2 = send(to_even, Z_EVEN), send(to_odd, Z_ODD)
    returned = [None, None]
    returned[1], mark = chip(1)
    near = kernel_call(
        text_grad_body, [((NEAR, WIDTH), F32)], [weights, image_all], flops=10 * UNIT_FLOPS, limit=16,
        after=[mark, opposite],
    )[0]
    to_even, to_odd = hop(0, 2, odd_2), hop(1, 2, even_2)
    even_3, odd_3 = send(to_even, Z_EVEN), send(to_odd, Z_ODD)
    returned[0], mark = chip(0, after=[to_even, to_odd])
    to_side = kernel_call(
        side_body, [CODE2], [keep[0], crossed[1], *returned[1]], final=True, flops=300 * UNIT_FLOPS
    )[0]
    from_side = send(to_side, SIDE)
    to_even, to_odd = hop(0, 1, odd_3, CODE, final=True), hop(1, 1, even_3, CODE, final=True)
    even_4, odd_4 = send(to_even, Z_EVEN), send(to_odd, Z_ODD)
    image_part = kernel_call(
        image_sum_body, [((ROWS, WIDTH), F32)], [keep[0], crossed[0], *returned[0]]
    )[0]
    loss = kernel_call(
        loss_ring_body,
        [((8, 128), F32)],
        [place, loss, opposite, even_1, odd_1, even_2, odd_2, even_3, odd_3],
        after=[to_odd, image_part],
    )[0]
    grad_images, images_done = kernel_call(
        image_final_body,
        [((ROWS, WIDTH), F32), ((8, 128), F32)],
        [scale, image_part, from_side],
        final=True,
    )
    grad_texts, texts_done = kernel_call(
        text_final_body,
        [((ROWS, WIDTH), F32), ((8, 128), F32)],
        [scale, near, even_3, odd_3, even_4, odd_4],
        final=True,
    )
    parts = kernel_call(
        loss_side_body, [LOSSES], [loss, send(loss, SIDE)], final=True, after=[images_done, texts_done]
    )[0]
    parts = exchange(parts, "loop")
    loss = kernel_call(loss_final_body, [((1,), F32)], [parts], final=True)[0]
    return loss, grad_images, grad_texts


def solution(mesh):
    rows = P(AXES, None)
    return jax.shard_map(
        on_device,
        mesh=mesh,
        in_specs=(rows, rows, P(AXES), P(), P()),
        out_specs=(P(), rows, rows),
        check_vma=False,
    )
```

```python
import functools
import jax
import jax.numpy as jnp
from jax import lax
from jax.experimental import pallas as pl
from jax.experimental.pallas import tpu as pltpu
from jax.sharding import PartitionSpec as P

AXES = ("loop", "inner")
N_LOOP, N_INNER = 16, 16
N_Z = 8
ROWS = 128
HALF = 64
WIDTH = 1536
CODE_WIDTH = WIDTH + 128
GROUPS = 5
IMAGES = GROUPS * 2 * ROWS
TEXTS = N_Z * ROWS
NEAR = 3 * ROWS
EARLY = 5 * ROWS
LATE = 7 * ROWS
TOP = slice(0, HALF)
BOTTOM = slice(HALF, ROWS)
MIB = 1024 * 1024


def pairs(move):
    out = []
    for loop in range(N_LOOP):
        for inner in range(N_INNER):
            chip, core, z, side = loop // 2, loop % 2, inner // 2, inner % 2
            to_chip, to_core, to_z, to_side = move(chip, core, z, side)
            out.append(
                (
                    loop * N_INNER + inner,
                    ((to_chip % 8) * 2 + to_core) * N_INNER + (to_z % N_Z) * 2 + to_side,
                )
            )
    return out


def across_edge(index, first):
    return index + 1 if index % 2 == first else index - 1


Z_EVEN = pairs(lambda c, k, z, s: (c, k, across_edge(z, 0), s))
Z_ODD = pairs(lambda c, k, z, s: (c, k, across_edge(z, 1), s))
CHIP_EVEN = pairs(lambda c, k, z, s: (across_edge(c, 0), k, z, s))
CHIP_ODD = pairs(lambda c, k, z, s: (across_edge(c, 1), k, z, 1 - s if c % 4 in (0, 3) else s))
SIDE = pairs(lambda c, k, z, s: (c, k, z, 1 - s))
CORE = pairs(lambda c, k, z, s: (c, 1 - k, z, s))
def send(array, route):
    return lax.ppermute(array, AXES, route)


Z_FLIP_4 = pairs(lambda c, k, z, s: (c, k, z ^ 4, s))


def exchange(parts, axis):
    parts = parts.reshape(N_LOOP, 8, 128)
    return lax.all_to_all(parts, axis, 0, 0, tiled=True).reshape(8 * N_LOOP, 128)


def vmem(array):
    return pltpu.with_memory_space_constraint(array, pltpu.VMEM)


VM = pl.BlockSpec(memory_space=pltpu.VMEM)
SM = pl.BlockSpec(memory_space=pltpu.SMEM)


def kernel_call(body, outs, args, scratch=(), aliases=None, flops=0, limit=8, after=(), final=False):
    count = len(args)

    def run(*refs):
        body(*refs[:count], *refs[count + len(after) :])

    place = jax.ShapeDtypeStruct if final else pltpu.VMEM
    return pl.pallas_call(
        run,
        out_shape=tuple(place(s, d) for s, d in outs),
        in_specs=[SM if a.ndim == 1 else VM for a in args] + [pl.BlockSpec(memory_space=pl.ANY)] * len(after),
        out_specs=tuple(SM if len(s) == 1 else VM for s, _ in outs),
        scratch_shapes=list(scratch),
        input_output_aliases=aliases or {},
        compiler_params=pltpu.CompilerParams(vmem_limit_bytes=limit * MIB),
        cost_estimate=pl.CostEstimate(flops=flops, bytes_accessed=0, transcendentals=0),
    )(*[a if a.ndim == 1 or final else vmem(a) for a in args], *after)


def encode(value, code_ref, rows, digits=None):
    top = jnp.max(jnp.abs(value), axis=1, keepdims=True)
    power = jnp.floor(jnp.log2(jnp.maximum(top, 1e-30))) - 13.0
    code = jnp.round(value * jnp.exp2(-power)).astype(jnp.int32)
    code_ref[rows, :WIDTH] = code.astype(jnp.int16)
    added = jnp.broadcast_to(power.astype(jnp.int32), (value.shape[0], 128))
    if digits is not None:
        lane = lax.broadcasted_iota(jnp.int32, added.shape, 1)
        added = jnp.where(lane < 32, added, jnp.broadcast_to(digits, added.shape))
    code_ref[rows, WIDTH:] = added.astype(jnp.int16)


def to_digits(total):
    power = jnp.floor(jnp.log2(jnp.maximum(total, 1e-30))) - 13.0
    scaled = total * jnp.exp2(-power)
    high = jnp.floor(scaled)
    low = jnp.round((scaled - high) * 8192.0)
    lane = lax.broadcasted_iota(jnp.int32, total.shape, 1)
    return jnp.where(lane < 64, power, jnp.where(lane < 96, high, low)).astype(jnp.int32)


def read_digits(code_ref):
    return code_ref[:16, WIDTH:].astype(jnp.int32)[:1, :]


def from_digits(digits):
    power, high, low = (digits[:, at : at + 1].astype(jnp.float32) for at in (32, 64, 96))
    return (high + low * (1.0 / 8192.0)) * jnp.exp2(power)


def decode(code_ref, rows):
    power = code_ref[rows, WIDTH:].astype(jnp.int32).astype(jnp.float32)[:, :1]
    return code_ref[rows, :WIDTH].astype(jnp.int32).astype(jnp.float32) * jnp.exp2(power)


def pair_terms(logits, positive):
    signed = logits if positive is None else jnp.where(positive, -logits, logits)
    small = jnp.exp(-jnp.abs(signed))
    whole = 1.0 + small
    weight = jnp.where(signed >= 0, 1.0, small) / whole
    series = small * (1.0 - small * (0.5 - small * (1.0 / 3.0)))
    loss = jnp.maximum(signed, 0.0) + jnp.where(small < 0.01, series, jnp.log(whole))
    if positive is not None:
        weight = jnp.where(positive, -weight, weight)
    return loss, weight.astype(jnp.bfloat16)


def weigh(text, image_ref, out_ref, base, groups, scale, bias, labels, scores):
    rows = text.shape[0]
    total = jnp.zeros((8, 256), jnp.float32)
    for group in groups:
        columns = slice(group * 256, group * 256 + 256)
        scores[:rows] = lax.dot_general(
            text, image_ref[columns, :], (((1,), (1,)), ((), ())), preferred_element_type=jnp.float32
        )
        for start in range(0, rows, 64):
            logits = scale * scores[start : start + 64] + bias
            positive = None
            if labels is not None and group == 0 and start < ROWS:
                row = start + lax.broadcasted_iota(jnp.int32, (64, 256), 0)
                positive = row == jnp.concatenate([labels, jnp.full_like(labels, -1)], axis=1)
            loss, weight = pair_terms(logits, positive)
            out_ref[base + start : base + start + 64, columns] = weight
            total = total + jnp.sum(loss.reshape(8, 8, 256), axis=0)
    return total[:, :128] + total[:, 128:]


def pass_body(array, out):
    del array, out


def choose_body(place, even0, even1, odd0, odd1, out):
    @pl.when(lax.rem(place[0], 2) == 0)
    def _():
        out[:ROWS, :] = even0[...]
        out[ROWS:, :] = even1[...]

    @pl.when(lax.rem(place[0], 2) != 0)
    def _():
        out[:ROWS, :] = odd0[...]
        out[ROWS:, :] = odd1[...]


def third_body(even, odd, even_out, odd_out):
    even_out[...] = even[HALF:, :]
    odd_out[...] = odd[:HALF, :]


def early_body(scale, bias, labels, *refs):
    images, texts = refs[:8], refs[8:13]
    weights, image_all, text_all, loss, scores = refs[13:]
    for i, ref in enumerate(images):
        image_all[i * ROWS : i * ROWS + ROWS, :] = ref[...]
    for i, ref in enumerate(texts):
        text_all[i * ROWS : i * ROWS + ROWS, :] = ref[...]
    loss[...] = weigh(
        text_all[:EARLY, :], image_all, weights, 0, range(4), scale[0], bias[0], labels[...], scores
    )


def middle_body(scale, bias, even, odd, across, loss_in, weights_in, image_in, text_in, weights, image_all, text_all, loss, scores):
    del weights_in, image_in, text_in
    text_all[EARLY : EARLY + ROWS, :] = even[...]
    text_all[EARLY + ROWS : LATE, :] = odd[...]
    image_all[8 * ROWS :, :] = across[...]
    loss[...] = (
        loss_in[...]
        + weigh(
            text_all[EARLY:LATE, :], image_all, weights, EARLY, range(4), scale[0], bias[0], None, scores
        )
        + weigh(text_all[:LATE, :], image_all, weights, 0, (4,), scale[0], bias[0], None, scores)
    )


def late_body(scale, bias, first, second, image_all, loss_in, weights_in, text_in, weights, text_all, loss, code_even, code_odd, far, scores):
    del weights_in, text_in
    text_all[LATE : LATE + HALF, :] = first[...]
    text_all[LATE + HALF :, :] = second[...]
    total = jnp.sum(
        loss_in[...]
        + weigh(
            text_all[LATE:, :], image_all, weights, LATE, range(GROUPS), scale[0], bias[0], None, scores
        )
    )
    digits = to_digits(jnp.full((1, 128), total, jnp.float32))
    loss[...] = jnp.broadcast_to(from_digits(digits), (8, 128))
    grad = jnp.dot(weights[NEAR:, :], image_all[...], preferred_element_type=jnp.float32)
    far[...] = grad[: 4 * ROWS]
    encode(grad[4 * ROWS : 4 * ROWS + HALF], code_even, TOP, digits)
    encode(grad[2 * ROWS : 2 * ROWS + HALF], code_even, BOTTOM, digits)
    encode(grad[4 * ROWS + HALF :], code_odd, TOP, digits)
    encode(grad[3 * ROWS + HALF : 4 * ROWS], code_odd, BOTTOM, digits)


def text_grad_body(weights, image_all, out):
    out[...] = jnp.dot(
        weights[:NEAR, :], image_all[...], preferred_element_type=jnp.float32
    )


def hop_body(top, bottom, top_part, bottom_part, code, out):
    digits = read_digits(code)
    encode(top_part[top : top + HALF, :] + decode(code, TOP), out, TOP, digits)
    if out.shape[0] > HALF:
        encode(bottom_part[bottom : bottom + HALF, :] + decode(code, BOTTOM), out, BOTTOM, digits)


def text_final_body(scale, part, third_even, third_odd, fourth_even, fourth_odd, out, done):
    done[...] = jnp.zeros((8, 128), jnp.float32)
    out[:HALF, :] = scale[0] * (
        part[:HALF, :] + decode(third_even, BOTTOM) + decode(fourth_odd, TOP)
    )
    out[HALF:, :] = scale[0] * (
        part[HALF:ROWS, :] + decode(third_odd, BOTTOM) + decode(fourth_even, TOP)
    )


def loss_sum(parts):
    total = parts[:8, :]
    for start in range(8, 8 * N_LOOP, 8):
        total = total + parts[start : start + 8, :]
    return total


def loss_ring_body(place, own, opposite, *refs):
    *codes, out = refs
    lane = lax.broadcasted_iota(jnp.int32, (8, 128), 1)
    z = lax.div(place[0], 2)
    step = 1 - 2 * lax.rem(z, 2)
    total = jnp.where(lane == z, own[...], 0.0)
    total = total + jnp.where(lane == lax.rem(z + 4, N_Z), opposite[...], 0.0)
    for i, code in enumerate(codes):
        distance = (i // 2 + 1) * (1 - 2 * (i % 2))
        other = lax.rem(z + step * distance + N_Z, N_Z)
        value = jnp.broadcast_to(from_digits(read_digits(code)), (8, 128))
        total = total + jnp.where(lane == other, value, 0.0)
    out[...] = total


def loss_side_body(one, two, out):
    total = one[...] + two[...]
    for i in range(N_LOOP):
        out[8 * i : 8 * i + 8, :] = total


def loss_final_body(parts, out):
    count = float(N_LOOP * N_INNER * ROWS) * float(GROUPS * N_INNER * ROWS)
    out[0] = jnp.sum(loss_sum(parts)[:1, :]) / count


def image_grad(weights, text_all, group):
    return lax.dot_general(
        weights[:, group * 256 : group * 256 + 256],
        text_all[...],
        (((0,), (0,)), ((), ())),
        preferred_element_type=jnp.float32,
    )


def image_code_body(weights, text_all, *outs):
    for i, group in enumerate((1, 4)):
        grad = image_grad(weights, text_all, group)
        for slot in range(2):
            encode(grad[slot * ROWS : slot * ROWS + ROWS], outs[slot], slice(i * ROWS, i * ROWS + ROWS))


def image_keep_body(weights, text_all, own, even, odd):
    for group, ref in ((0, own), (2, even), (3, odd)):
        ref[...] = image_grad(weights, text_all, group)


def chip_body(slot, place, even, odd, code, even_out, odd_out):
    rows = slice(slot * ROWS, slot * ROWS + ROWS)
    extra = decode(code, slice(ROWS, 2 * ROWS))
    first = (lax.rem(place[0], 2) == 0).astype(jnp.float32)
    encode(even[rows, :] + first * extra, even_out, slice(0, ROWS))
    encode(odd[rows, :] + (1.0 - first) * extra, odd_out, slice(0, ROWS))


def side_body(own, other, one, two, out):
    rows = slice(0, ROWS)
    encode(
        own[ROWS:, :] + decode(other, rows) + decode(one, rows) + decode(two, rows), out, rows
    )


def image_sum_body(own, other, one, two, out):
    rows = slice(0, ROWS)
    out[...] = own[:ROWS, :] + decode(other, rows) + decode(one, rows) + decode(two, rows)


def image_final_body(scale, part, side, out, done):
    done[...] = jnp.zeros((8, 128), jnp.float32)
    out[...] = scale[0] * (part[...] + decode(side, slice(0, ROWS)))


CODE = ((HALF, CODE_WIDTH), jnp.int16)
CODE2 = ((ROWS, CODE_WIDTH), jnp.int16)
CODE4 = ((2 * ROWS, CODE_WIDTH), jnp.int16)
BF, F32 = jnp.bfloat16, jnp.float32
UNIT_FLOPS = 2 * ROWS * ROWS * WIDTH
LOSSES = ((8 * N_LOOP, 128), F32)


def on_device(images, texts, labels, scale, bias):
    loop = lax.axis_index("loop")
    place = (
        2 * lax.div(lax.axis_index("inner"), 2) + lax.rem(loop + lax.div(loop, 2), 2)
    ).reshape(1)
    even_1, odd_1 = send(texts, Z_EVEN), send(texts, Z_ODD)
    own = [images, send(images, SIDE)]
    chip_even, chip_odd = [send(images, CHIP_EVEN)], [send(images, CHIP_ODD)]
    own[1] = kernel_call(
        pass_body, [((ROWS, WIDTH), BF)], [own[1]], aliases={0: 0}, after=[chip_even[0], chip_odd[0]]
    )[0]
    chip_even.append(send(own[1], CHIP_EVEN))
    chip_odd.append(send(own[1], CHIP_ODD))
    even_2, odd_2 = send(odd_1, Z_EVEN), send(even_1, Z_ODD)
    other = [send(a, CORE) for a in own]
    even_3, odd_3 = send(odd_2, Z_EVEN), send(even_2, Z_ODD)
    across = send(
        kernel_call(choose_body, [((2 * ROWS, WIDTH), BF)], [place, *chip_even, *chip_odd])[0], CORE
    )
    weights, image_all, text_all, loss = kernel_call(
        early_body,
        [((TEXTS, IMAGES), BF), ((IMAGES, WIDTH), BF), ((TEXTS, WIDTH), BF), ((8, 128), F32)],
        [scale, bias, labels.reshape(1, ROWS), *own, *other, *chip_even, *chip_odd]
        + [texts, even_1, odd_1, even_2, odd_2],
        scratch=[pltpu.VMEM((EARLY, 256), F32)],
        flops=40 * UNIT_FLOPS,
        limit=16,
    )
    last_even, last_odd = kernel_call(
        third_body, [((HALF, WIDTH), BF)] * 2, [even_3, odd_3], flops=60 * UNIT_FLOPS, after=[loss]
    )
    even_4, odd_4 = send(last_odd, Z_EVEN), send(last_even, Z_ODD)
    weights, image_all, text_all, loss = kernel_call(
        middle_body,
        [((TEXTS, IMAGES), BF), ((IMAGES, WIDTH), BF), ((TEXTS, WIDTH), BF), ((8, 128), F32)],
        [scale, bias, even_3, odd_3, across, loss, weights, image_all, text_all],
        scratch=[pltpu.VMEM((LATE, 256), F32)],
        aliases={6: 0, 7: 1, 8: 2},
        flops=30 * UNIT_FLOPS,
        limit=16,
    )
    weights, text_all, loss, code_even, code_odd, far = kernel_call(
        late_body,
        [((TEXTS, IMAGES), BF), ((TEXTS, WIDTH), BF), ((8, 128), F32), CODE2, CODE2, ((4 * ROWS, WIDTH), F32)],
        [scale, bias, even_4, odd_4, image_all, loss, weights, text_all],
        scratch=[pltpu.VMEM((ROWS, 256), F32)],
        aliases={6: 0, 7: 1},
        flops=40 * UNIT_FLOPS,
        limit=16,
    )
    even_1, odd_1 = send(code_even, Z_EVEN), send(code_odd, Z_ODD)
    opposite = send(loss, Z_FLIP_4)
    codes = kernel_call(
        image_code_body, [CODE4] * 2, [weights, text_all], flops=8 * UNIT_FLOPS, limit=16,
        after=[code_even],
    )
    crossed = [send(code, CORE) for code in codes]
    keep = kernel_call(
        image_keep_body,
        [((256, WIDTH), F32)] * 3,
        [weights, text_all],
        flops=10 * UNIT_FLOPS,
        limit=16,
        after=[codes[0]],
    )

    def hop(way, step, code, out=CODE2, after=(), final=False):
        half = HALF * ((step + way) % 2)
        parts = []
        for at in (step, step - 1):
            if at >= 2:
                parts.append((far, (2 * at - 4 + way) * ROWS + half))
            else:
                parts.append((near, max(2 * at - 1 + way, 0) * ROWS + half))
        (one, top), (two, bottom) = parts
        return kernel_call(
            functools.partial(hop_body, top, bottom), [out], [one, two, code],
            flops=400 * UNIT_FLOPS, final=final, after=after,
        )[0]

    def chip(slot, after=()):
        to_even, to_odd = kernel_call(
            functools.partial(chip_body, slot), [CODE2] * 2, [place, keep[1], keep[2], crossed[slot]],
            flops=300 * UNIT_FLOPS, after=after,
        )
        return [send(to_even, CHIP_EVEN), send(to_odd, CHIP_ODD)], to_odd

    to_even, to_odd = hop(0, 3, odd_1), hop(1, 3, even_1)
    even_2, odd_2 = send(to_even, Z_EVEN), send(to_odd, Z_ODD)
    returned = [None, None]
    returned[1], mark = chip(1)
    near = kernel_call(
        text_grad_body, [((NEAR, WIDTH), F32)], [weights, image_all], flops=10 * UNIT_FLOPS, limit=16,
        after=[mark, opposite],
    )[0]
    to_even, to_odd = hop(0, 2, odd_2), hop(1, 2, even_2)
    even_3, odd_3 = send(to_even, Z_EVEN), send(to_odd, Z_ODD)
    returned[0], mark = chip(0, after=[to_even, to_odd])
    to_side = kernel_call(
        side_body, [CODE2], [keep[0], crossed[1], *returned[1]], final=True, flops=300 * UNIT_FLOPS
    )[0]
    from_side = send(to_side, SIDE)
    to_even, to_odd = hop(0, 1, odd_3, CODE, final=True), hop(1, 1, even_3, CODE, final=True)
    even_4, odd_4 = send(to_even, Z_EVEN), send(to_odd, Z_ODD)
    image_part = kernel_call(
        image_sum_body, [((ROWS, WIDTH), F32)], [keep[0], crossed[0], *returned[0]]
    )[0]
    loss = kernel_call(
        loss_ring_body,
        [((8, 128), F32)],
        [place, loss, opposite, even_1, odd_1, even_2, odd_2, even_3, odd_3],
        after=[to_odd, image_part],
    )[0]
    grad_images, images_done = kernel_call(
        image_final_body,
        [((ROWS, WIDTH), F32), ((8, 128), F32)],
        [scale, image_part, from_side],
        final=True,
    )
    grad_texts, _ = kernel_call(
        text_final_body,
        [((ROWS, WIDTH), F32), ((8, 128), F32)],
        [scale, near, even_3, odd_3, even_4, odd_4],
        final=True,
    )
    parts = kernel_call(
        loss_side_body, [LOSSES], [loss, send(loss, SIDE)], final=True, after=[images_done]
    )[0]
    parts = exchange(parts, "loop")
    loss = kernel_call(loss_final_body, [((1,), F32)], [parts], final=True)[0]
    return loss, grad_images, grad_texts


def solution(mesh):
    rows = P(AXES, None)
    return jax.shard_map(
        on_device,
        mesh=mesh,
        in_specs=(rows, rows, P(AXES), P(), P()),
        out_specs=(P(), rows, rows),
        check_vma=False,
    )
```
